128 devices in a mesh: leaf: 8 (over z, core), sub: 16 (over x, y).
Axes of the slice: x: 4, y: 4, z: 4, core: 2. Of those that a mesh axis runs over, the one named last changes fastest.
Arguments:
- leaf_matrix: float32 [128, 512, 512], P(('leaf', 'sub')), may hold values from 0 to 4, as said below
- leaf_source: float32 [128, 512], P(('leaf', 'sub')), may hold values from -6 to 6
- observe: float32 [128, 512], P(('leaf', 'sub')), may hold values from -6 to 6
- zone_ids: int32 [128, 512], P(('leaf', 'sub')), may hold values from 0 to 16383
- log_perm: float32 [16384], P(('leaf', 'sub')), may hold values from -1 to 1
- block_map: int32 [254, 4], replicated, may hold values from 0 to 6, as said below
Outputs:
- leaf_solution: float32 [128, 512], P(('leaf', 'sub'))
- gradient: float32 [16384], P(('leaf', 'sub'))
The draws below stay inside these ranges and needn't reach their ends.
Inputs may be any that keep to these rules, and one draw needn't show every extreme that they name: `block_map`: rows 2q and 2q + 1 (sibling nodes) each hold 4 distinct blocks; together they name every value from 0 to 6, sharing exactly one. Each leaf_matrix[d] is symmetric and positive definite.
All inputs are finite; a program needn't handle non-finite values.
Results may differ from the reference program's by a relative error of at most 0.0003.
Values sent between devices are 32-bit elements; how exact they have to be, the bound alone decides.
No kernel may reach another device: no remote copies, remote signals or barrier semaphores. Data moves between devices by JAX's collectives and lax.ppermute only.
A program may use at most 128 MiB of HBM per device.

```python
import math
import jax
import jax.numpy as jnp
from jax import lax

NBLK = 4
FRONT = 512
ZONES = 16384
N_LEAF = 8
N_SUB = 16


def kernel_matrix(place_key, device_count, reach):
    places = jax.random.uniform(place_key, (device_count, 3, FRONT), jnp.float32, 0.0, 1.0)
    length_scale = (reach / (8.0 * math.pi * FRONT)) ** (1.0 / 3.0)
    squared = jnp.zeros((device_count, FRONT, FRONT), jnp.float32)
    for coord_index in range(3):
        column = places[:, coord_index, :]
        between = column[:, :, None] - column[:, None, :]
        squared = squared + between * between
    return jnp.exp(-jnp.sqrt(squared) / length_scale)


def draw_leaf_matrix(key, part):
    key = jax.random.fold_in(key, 11)
    place_key, diag_key = jax.random.split(key)
    device_count = N_LEAF * N_SUB
    kernel = kernel_matrix(place_key, device_count, 24.0)
    diagonal = jax.random.uniform(diag_key, (device_count, FRONT), jnp.float32, 0.25, 0.75)
    identity = jnp.eye(FRONT, dtype=jnp.float32)
    return 3.0 * kernel + identity * diagonal[:, :, None]


def draw_block_map(key, part):
    key = jax.random.fold_in(key, 23)
    pair_count = N_LEAF * N_SUB - 1
    parent_blocks = 2 * NBLK - 1
    orders = jax.vmap(lambda one_key: jax.random.permutation(one_key, parent_blocks))(jax.random.split(key, pair_count))
    orders = orders.astype(jnp.int32)
    return jnp.stack([orders[:, :NBLK], orders[:, NBLK - 1:]], axis=1).reshape(2 * pair_count, NBLK)


def set_ends(values, rng, smallest, largest):
    index_at = [jax.random.randint(jax.random.fold_in(rng, axis), (), 0, length) for axis, length in enumerate(values.shape)]
    main_axis = values.shape.index(max(values.shape))
    beside = index_at[:main_axis] + [(index_at[main_axis] + 1) % values.shape[main_axis]] + index_at[main_axis + 1:]
    return values.at[tuple(index_at)].set(smallest).at[tuple(beside)].set(largest)


def block_scale(key, shape, pieces, smallest, top_value):
    def one(position, shards_of):
        steps = jax.random.uniform(jax.random.fold_in(jax.random.fold_in(key, 6), position), (shards_of,), jnp.float32, smallest / len(pieces), top_value / len(pieces))
        return jnp.repeat(jnp.exp(steps), shape[position] // shards_of).reshape((-1,) + (1,) * (len(shape) - position - 1))

    gain = one(*pieces[0])
    for cut in pieces[1:]:
        gain = gain * one(*cut)
    return gain


def centred(rng, extent, width, most, cuts=(), kind=jnp.bfloat16):
    level = block_scale(rng, extent, cuts, -0.22, 0.18) if cuts else 1.0
    array = jax.random.normal(rng, extent, jnp.float32) * width * level
    return jnp.minimum(jnp.maximum(array, -most), most).astype(kind)


def setup_inputs(seed: int = 0) -> dict:
    seeds = jax.random.split(jax.random.key(seed), 7)
    leaf_matrix = draw_leaf_matrix(jax.random.fold_in(seeds[6], 71), 0)
    leaf_source = centred(seeds[1], (N_LEAF * N_SUB, FRONT), 1.0, 6.0, ((0, 128),), jnp.float32)
    observe = centred(seeds[2], (N_LEAF * N_SUB, FRONT), 1.0, 6.0, ((0, 128),), jnp.float32)
    zone_ids = set_ends(jax.random.randint(seeds[3], (N_LEAF * N_SUB, FRONT), 0, ZONES), jax.random.fold_in(seeds[3], 1), 0, ZONES - 1).astype(jnp.int32)
    log_perm = jnp.clip(jax.random.uniform(seeds[4], (ZONES,), jnp.float32, -1.0, 1.0) * block_scale(seeds[4], (ZONES,), ((0, 128),), -0.4, 0.0), -1.0, 1.0)
    block_map = draw_block_map(jax.random.fold_in(seeds[6], 71), 0)
    return dict(leaf_matrix=leaf_matrix, leaf_source=leaf_source, observe=observe, zone_ids=zone_ids, log_perm=log_perm, block_map=block_map)


EXACT_ARITHMETIC = lax.Precision.HIGHEST

def lower_triangle_solve(front_factor, rhs, transpose=False):
    return lax.linalg.triangular_solve(front_factor, rhs, left_side=True, lower=True, transpose_a=transpose)

def selector(block_rows, parent_blocks):
    return (jnp.arange(parent_blocks, dtype=jnp.int32)[:, None] == block_rows.astype(jnp.int32)[None, :]).astype(jnp.float32)

def extend_add(matrix, right_vector, block_rows):
    block_count = block_rows.shape[0]
    block_width = matrix.shape[0] // block_count
    parent_blocks = 2 * block_count - 1
    chooser = selector(block_rows, parent_blocks)
    blocked = matrix.reshape(block_count, block_width, block_count, block_width)
    blocked = jnp.einsum('pi,iajb->pajb', chooser, blocked, precision=EXACT_ARITHMETIC)
    blocked = jnp.einsum('pajb,qj->paqb', blocked, chooser, precision=EXACT_ARITHMETIC)
    spread = jnp.einsum('pi,kia->kpa', chooser, right_vector.reshape(2, block_count, block_width), precision=EXACT_ARITHMETIC)
    parent_size = parent_blocks * block_width
    return (blocked.reshape(parent_size, parent_size), spread.reshape(2, parent_size))

def eliminate(parent_node, right_vector, frontal_width):
    elimination_count = parent_node.shape[0] - frontal_width
    front_factor = jnp.linalg.cholesky(parent_node[:elimination_count, :elimination_count])
    interface_coupling = lower_triangle_solve(front_factor, parent_node[:elimination_count, elimination_count:])
    reduced_system = lower_triangle_solve(front_factor, right_vector[:, :elimination_count].T)
    schur_complement = parent_node[elimination_count:, elimination_count:] - jnp.dot(interface_coupling.T, interface_coupling, precision=EXACT_ARITHMETIC)
    updated_vector = right_vector[:, elimination_count:] - jnp.dot(interface_coupling.T, reduced_system, precision=EXACT_ARITHMETIC).T
    return (schur_complement, updated_vector, front_factor, interface_coupling, reduced_system)

def recover(front_factor, interface_coupling, reduced_system, kept_part):
    upper_part = lower_triangle_solve(front_factor, reduced_system - jnp.dot(interface_coupling, kept_part.T, precision=EXACT_ARITHMETIC), True)
    return jnp.concatenate([upper_part.T, kept_part], axis=1)

def restrict(solution, block_rows):
    block_count = block_rows.shape[0]
    parent_blocks = 2 * block_count - 1
    block_width = solution.shape[1] // parent_blocks
    chooser = selector(block_rows, parent_blocks)
    picked = jnp.einsum('pi,kpa->kia', chooser, solution.reshape(2, parent_blocks, block_width), precision=EXACT_ARITHMETIC)
    return picked.reshape(2, block_count * block_width)

def reference(leaf_matrix, leaf_source, observe, zone_ids, log_perm, block_map):
    device_count = N_LEAF * N_SUB
    frontal_width = leaf_matrix.shape[-1]

    def to_tree(values_in):
        return jnp.swapaxes(values_in.reshape((N_LEAF, N_SUB) + values_in.shape[1:]), 0, 1).reshape(values_in.shape)

    def from_tree(values_in):
        return jnp.swapaxes(values_in.reshape((N_SUB, N_LEAF) + values_in.shape[1:]), 0, 1).reshape(values_in.shape)
    perm_diag = jnp.exp(log_perm[zone_ids])
    identity = jnp.eye(frontal_width, dtype=jnp.float32)
    matrices = to_tree(leaf_matrix + identity[None] * perm_diag[:, None, :])
    vectors = to_tree(jnp.stack([leaf_source, observe], axis=1))
    level_count = device_count.bit_length() - 1
    stored = []
    node_count = device_count
    for level_index in range(level_count):
        map_rows = block_map[node_count - 2:2 * node_count - 2]
        pairs = node_count // 2

        def combine(inputs):
            pair_mats, pair_vecs, pair_rows = inputs
            first_m, first_v = extend_add(pair_mats[0], pair_vecs[0], pair_rows[0])
            second_m, second_v = extend_add(pair_mats[1], pair_vecs[1], pair_rows[1])
            return eliminate(first_m + second_m, first_v + second_v, frontal_width)
        result = lax.map(combine, (matrices.reshape(pairs, 2, frontal_width, frontal_width), vectors.reshape(pairs, 2, 2, frontal_width), map_rows.reshape(pairs, 2, -1)))
        matrices, vectors = (result[0], result[1])
        stored.append((result[2], result[3], result[4], map_rows.reshape(pairs, 2, -1)))
        node_count = pairs
    root_factor = jnp.linalg.cholesky(matrices[0])
    middle = lower_triangle_solve(root_factor, vectors[0].T)
    solution = lower_triangle_solve(root_factor, middle, True).T[None]
    for level_index in reversed(range(level_count)):
        factors, couplings, reduceds, pair_maps = stored[level_index]
        pairs = factors.shape[0]

        def expand(inputs):
            front_factor, interface_coupling, reduced_system, pair_rows, kept_part = inputs
            parent_sol = recover(front_factor, interface_coupling, reduced_system, kept_part)
            return jnp.stack([restrict(parent_sol, pair_rows[0]), restrict(parent_sol, pair_rows[1])])
        solution = lax.map(expand, (factors, couplings, reduceds, pair_maps, solution)).reshape(2 * pairs, 2, frontal_width)
    leaf_pair = from_tree(solution)
    leaf_solution = leaf_pair[:, 0]
    adjoint = leaf_pair[:, 1]
    terms = -perm_diag * leaf_solution * adjoint
    gradient = jax.ops.segment_sum(terms.reshape(-1), zone_ids.reshape(-1), num_segments=log_perm.shape[0])
    return (leaf_solution, gradient)
```

```python
import functools

import jax
import jax.numpy as jnp
from jax import lax
from jax.experimental import pallas as pl
from jax.experimental.pallas import tpu as pltpu
from jax.sharding import PartitionSpec as P

BW = 128
NB = 4
KEEP = NB - 1
FW = NB * BW
RHS = FW
SHARED = RHS + 8
ROWS = SHARED + BW
COLS = FW + BW
PAIRS = [(i, j) for i in range(NB) for j in range(i, NB)]
PACK = len(PAIRS) * BW + NB * 8
VMEM_LIMIT = 48 * 1024 * 1024


def split(x):
    high = x.astype(jnp.bfloat16)
    return high, (x - high.astype(jnp.float32)).astype(jnp.bfloat16)


def dot_split(a, b):
    one = functools.partial(jnp.dot, preferred_element_type=jnp.float32)
    return one(a[0], b[0]) + (one(a[0], b[1]) + one(a[1], b[0]))


def lanes(x, c):
    return jnp.broadcast_to(x[:, c : c + 1], (8, BW))


def rows(x, j):
    return jnp.broadcast_to(x[j : j + 1, :], (8, BW))


def invert(slabs):
    lane = lax.broadcasted_iota(jnp.int32, (8, BW), 1)
    sub = lax.broadcasted_iota(jnp.int32, (8, BW), 0)
    slabs = list(slabs)
    count = len(slabs)
    for k in range(count):
        cols = [lanes(slabs[k], 8 * k + j) for j in range(8)]
        inside = (lane >= 8 * k) & (lane < 8 * k + 8)
        row = jnp.where(lane == sub + 8 * k, 1.0, jnp.where(inside, 0.0, slabs[k]))
        for j in range(8):
            inv = 1.0 / rows(cols[j], j)
            w = rows(row, j) * inv
            row = jnp.where(sub == j, w, row - cols[j] * w)
            for m in range(j + 1, 8):
                cm = rows(cols[m], j) * inv
                cols[m] = jnp.where(sub == j, cm, cols[m] - cols[j] * cm)
        w = [rows(row, j) for j in range(8)]
        for r in list(range(k + 1, count)) + list(range(k)):
            t0 = jnp.where(inside, 0.0, slabs[r]) - lanes(slabs[r], 8 * k) * w[0]
            t1 = lanes(slabs[r], 8 * k + 1) * w[1]
            for j in range(2, 8, 2):
                t0 = t0 - lanes(slabs[r], 8 * k + j) * w[j]
                t1 = t1 + lanes(slabs[r], 8 * k + j + 1) * w[j + 1]
            slabs[r] = t0 - t1
        slabs[k] = row
    return slabs


def row_of(block):
    return jnp.where(block == NB, SHARED, block * BW)


def sweep(front, inverse, wide, block):
    ro = pl.multiple_of(row_of(block), 8)
    co = pl.multiple_of(block * BW, BW)
    out = invert([front[pl.ds(ro + 8 * r, 8), pl.ds(co, BW)] for r in range(BW // 8)])
    for r in range(BW // 8):
        inverse[8 * r : 8 * r + 8, :] = out[r]
    wide[...] = dot_split(split(inverse[...]), split(front[pl.ds(ro, BW), :]))
    wide[:, pl.ds(co, BW)] = inverse[...]
    w = split(wide[...])
    for at, size in [(i * BW, BW) for i in range(NB)] + [(RHS, 8)]:
        g = split(front[at : at + size, pl.ds(co, BW)])
        front[at : at + size, pl.ds(co, BW)] = jnp.zeros((size, BW), jnp.float32)
        front[at : at + size, :] -= dot_split(g, w)


def place(map_ref, row, other):
    mine = [map_ref[row * NB + i] for i in range(NB)]
    theirs = [map_ref[other * NB + i] for i in range(NB)]
    out = []
    for m in mine:
        both = functools.reduce(jnp.logical_or, [m == t for t in theirs])
        out.append(jnp.where(m >= KEEP, m - KEEP, jnp.where(both, NB, -1)))
    return out


def map_rows(tree, level, devices):
    nodes = devices >> level
    node = tree >> level
    return nodes + node - 2, nodes + (node ^ 1) - 2


def eliminate(front, inverse, wide, flags, blocks, pack):
    def step(n, carry):
        @pl.when(flags[n] == 1)
        def _():
            sweep(front, inverse, wide, lax.rem(n + NB, NB + 1))

        return carry

    lax.fori_loop(1 if blocks == NB else 0, NB + 1, step, 0)
    if pack is not None:
        for p, (i, j) in enumerate(PAIRS):
            pack[p * BW : p * BW + BW, :] = front[i * BW : i * BW + BW, j * BW : j * BW + BW]
        for i in range(NB):
            at = len(PAIRS) * BW + 8 * i
            pack[at : at + 8, :] = front[RHS : RHS + 8, i * BW : i * BW + BW]


def set_flags(flags, map_ref, tree, level, devices):
    if devices >> level == 1:
        for i in range(NB):
            flags[1 + i] = 1
        return
    for i, slot in enumerate(place(map_ref, *map_rows(tree, level, devices))):
        flags[1 + i] = jnp.where(slot < 0, 1, 0)


def leaf_kernel(devices, tree_ref, map_ref, leaf, source, observe, perm, front, pack, inverse, wide, flags):
    front[0:FW, :] = leaf[...]
    eye = lax.broadcasted_iota(jnp.int32, (BW, BW), 0) == lax.broadcasted_iota(jnp.int32, (BW, BW), 1)
    for i in range(NB):
        at = slice(i * BW, i * BW + BW)
        front[at, at] += jnp.where(eye, jnp.broadcast_to(perm[:, at], (BW, BW)), 0.0)
    which = lax.broadcasted_iota(jnp.int32, (8, FW), 0)
    front[RHS : RHS + 8, :] = jnp.where(
        which == 0,
        jnp.broadcast_to(source[...], (8, FW)),
        jnp.where(which == 1, jnp.broadcast_to(observe[...], (8, FW)), 0.0),
    )
    set_flags(flags, map_ref, tree_ref[0], 0, devices)
    eliminate(front, inverse, wide, flags, NB, pack)


def merge_kernel(devices, level, tree_ref, map_ref, own, theirs, front, *rest):
    pack = rest[0] if len(rest) == 5 else None
    inverse, wide, flags, slots = rest[-4:]
    tree = tree_ref[0]
    row, other = map_rows(tree, level, devices)
    mine, yours = place(map_ref, row, other), place(map_ref, other, row)
    flags[0] = functools.reduce(jnp.maximum, [jnp.where(s == NB, 1, 0) for s in mine])
    set_flags(flags, map_ref, tree, level + 1, devices)
    for i in range(NB):
        slots[i] = mine[i]
    front[...] = jnp.zeros(front.shape, jnp.float32)

    def one(p, carry):
        i, j = p // NB, lax.rem(p, NB)
        a, b = slots[i], slots[j]

        @pl.when((a >= 0) & (b >= 0))
        def _():
            front[pl.ds(pl.multiple_of(row_of(a), 8), BW), pl.ds(pl.multiple_of(b * BW, BW), BW)] = own[
                pl.ds(pl.multiple_of(i * BW, BW), BW), pl.ds(pl.multiple_of(j * BW, BW), BW)
            ]

        return carry

    lax.fori_loop(0, NB * NB, one, 0)
    for i in range(NB):

        @pl.when(mine[i] >= 0)
        def _():
            co = pl.ds(pl.multiple_of(mine[i] * BW, BW), BW)
            front[RHS : RHS + 8, co] = own[RHS : RHS + 8, i * BW : i * BW + BW]

    for p, (i, j) in enumerate(PAIRS):
        a, b = yours[i], yours[j]

        @pl.when((a >= 0) & (b >= 0))
        def _():
            block = theirs[p * BW : p * BW + BW, :]
            front[pl.ds(pl.multiple_of(row_of(a), 8), BW), pl.ds(pl.multiple_of(b * BW, BW), BW)] += block
            if i != j:
                front[pl.ds(pl.multiple_of(row_of(b), 8), BW), pl.ds(pl.multiple_of(a * BW, BW), BW)] += block.T

    for i in range(NB):

        @pl.when(yours[i] >= 0)
        def _():
            at = len(PAIRS) * BW + 8 * i
            front[RHS : RHS + 8, pl.ds(pl.multiple_of(yours[i] * BW, BW), BW)] += theirs[at : at + 8, :]

    eliminate(front, inverse, wide, flags, NB + 1, pack)


def recover_kernel(devices, levels, tree_ref, map_ref, *refs):
    fronts, out, kept, solved = refs[: levels + 1], refs[levels + 1], refs[levels + 2], refs[levels + 3]
    tree = tree_ref[0]
    solved[...] = -fronts[levels][RHS : RHS + 8, :]
    for level in reversed(range(levels)):
        front = fronts[level]
        slots = place(map_ref, *map_rows(tree, level, devices))
        for i in range(NB):
            at = slice(i * BW, i * BW + BW)
            kept[:, at] = jnp.zeros((8, BW), jnp.float32)

            @pl.when(slots[i] >= 0)
            def _():
                kept[:, at] = solved[:, pl.ds(pl.multiple_of(slots[i] * BW, BW), BW)]

        width = front.shape[1]
        new = dot_split(split(kept[...]), split(front[0:FW, :])) - front[RHS : RHS + 8, :]
        solved[:, 0:width] = new
        for i in range(NB):
            at = slice(i * BW, i * BW + BW)

            @pl.when(slots[i] >= 0)
            def _():
                solved[:, at] = kept[:, at]

    out[...] = solved[:, 0:FW]


SCALARS = pl.BlockSpec(memory_space=pltpu.SMEM)
WHOLE = pl.BlockSpec(memory_space=pltpu.VMEM)
PARAMS = pltpu.CompilerParams(vmem_limit_bytes=VMEM_LIMIT)


def f32(*shape):
    return jax.ShapeDtypeStruct(shape, jnp.float32)


def scratch(width):
    return [pltpu.VMEM((BW, BW), jnp.float32), pltpu.VMEM((BW, width), jnp.float32), pltpu.SMEM((8,), jnp.int32)]


def leaf_front(devices, tree, maps, leaf, source, observe, perm):
    return pl.pallas_call(
        functools.partial(leaf_kernel, devices),
        out_shape=(f32(SHARED, FW), f32(PACK, BW)),
        in_specs=[SCALARS, SCALARS] + [WHOLE] * 4,
        out_specs=(WHOLE, WHOLE),
        scratch_shapes=scratch(FW),
        compiler_params=PARAMS,
        name="leaf_front",
    )(tree, maps, leaf, source, observe, perm)


def merge(devices, level, tree, maps, own, theirs):
    last = devices >> (level + 1) == 1
    out = (f32(ROWS, COLS),) + (() if last else (f32(PACK, BW),))
    result = pl.pallas_call(
        functools.partial(merge_kernel, devices, level),
        out_shape=out,
        in_specs=[SCALARS, SCALARS, WHOLE, WHOLE],
        out_specs=(WHOLE,) * len(out),
        scratch_shapes=scratch(COLS) + [pltpu.SMEM((8,), jnp.int32)],
        compiler_params=PARAMS,
        name=f"merge_{level}",
    )(tree, maps, own, theirs)
    return result if not last else (result[0], None)


def recover(devices, tree, maps, fronts):
    return pl.pallas_call(
        functools.partial(recover_kernel, devices, len(fronts) - 1),
        out_shape=f32(8, FW),
        in_specs=[SCALARS, SCALARS] + [WHOLE] * len(fronts),
        out_specs=WHOLE,
        scratch_shapes=[pltpu.VMEM((8, FW), jnp.float32), pltpu.VMEM((8, COLS), jnp.float32)],
        compiler_params=PARAMS,
        name="recover",
    )(tree, maps, *fronts)


def partner(block, axis, bit):
    count = lax.axis_size(axis)
    return lax.ppermute(block, axis, [(k, k ^ (1 << bit)) for k in range(count)])


def shards(leaf_matrix, leaf_source, observe, zone_ids, log_perm, block_map):
    leaf_count = lax.axis_size("leaf")
    sub_count = lax.axis_size("sub")
    devices = leaf_count * sub_count
    leaf_bits = leaf_count.bit_length() - 1
    levels = devices.bit_length() - 1
    tree = (lax.axis_index("leaf") + leaf_count * lax.axis_index("sub")).astype(jnp.int32)[None]
    maps = block_map.reshape(-1)
    all_zones = lax.all_gather(log_perm, ("leaf", "sub"), axis=0, tiled=True)
    cells = zone_ids[0]
    perm = jnp.exp(all_zones[cells])
    front, pack = leaf_front(devices, tree, maps, leaf_matrix[0], leaf_source, observe, perm[None])
    fronts = [front]
    for level in range(levels):
        axis, bit = ("leaf", level) if level < leaf_bits else ("sub", level - leaf_bits)
        front, pack = merge(devices, level, tree, maps, front, partner(pack, axis, bit))
        fronts.append(front)
    solution = recover(devices, tree, maps, fronts)
    terms = -perm * solution[0] * solution[1]
    partial = jax.ops.segment_sum(terms, cells, num_segments=all_zones.shape[0])
    gradient = lax.psum_scatter(partial, ("leaf", "sub"), scatter_dimension=0, tiled=True)
    return solution[0][None, :], gradient


def solution(mesh):
    split_all = ("leaf", "sub")
    in_specs = (P(split_all, None, None), P(split_all, None), P(split_all, None), P(split_all, None), P(split_all), P())
    out_specs = (P(split_all, None), P(split_all))
    return jax.shard_map(shards, mesh=mesh, in_specs=in_specs, out_specs=out_specs, check_vma=False)
```

```python
import functools

import jax
import jax.numpy as jnp
from jax import lax
from jax.experimental import pallas as pl
from jax.experimental.pallas import tpu as pltpu
from jax.sharding import PartitionSpec as P

BW = 128
NB = 4
KEEP = NB - 1
FW = NB * BW
RHS = FW
SHARED = RHS + 8
ROWS = SHARED + BW
COLS = FW + BW
PAIRS = [(i, j) for i in range(NB) for j in range(i, NB)]
HALF_PAIRS, HALF_RHS = len(PAIRS) // 2, NB // 2
HALF = HALF_PAIRS * BW + HALF_RHS * 8
VMEM_LIMIT = 48 * 1024 * 1024


def split(x):
    high = x.astype(jnp.bfloat16)
    return high, (x - high.astype(jnp.float32)).astype(jnp.bfloat16)


def dot_split(a, b):
    one = functools.partial(jnp.dot, preferred_element_type=jnp.float32)
    both = one(jnp.concatenate([a[0], a[1]], 1), jnp.concatenate([b[0], b[0]], 0))
    return both + one(a[0], b[1])


def lanes(x, c):
    return jnp.broadcast_to(x[:, c : c + 1], (8, BW))


def rows(x, j):
    return jnp.broadcast_to(x[j : j + 1, :], (8, BW))


def pivots(row, cols, sub):
    for j in range(0, 8, 2):
        left, right = cols[j], cols[j + 1]
        a, b, c = rows(left, j), rows(left, j + 1), rows(right, j + 1)
        scale = 1.0 / (a * c - b * b)
        first, second = sub == j, sub == j + 1

        def update(v):
            v0, v1 = rows(v, j), rows(v, j + 1)
            u0 = c * v0 - b * v1
            u1 = a * v1 - b * v0
            t = left * u0 + right * u1
            return jnp.where(first, u0 * scale, jnp.where(second, u1 * scale, v - t * scale))

        row = update(row)
        for m in range(j + 2, 8):
            cols[m] = update(cols[m])
    return row


def invert(slabs):
    lane = lax.broadcasted_iota(jnp.int32, (8, BW), 1)
    sub = lax.broadcasted_iota(jnp.int32, (8, BW), 0)
    slabs = list(slabs)
    count = len(slabs)
    half = count // 2
    for panel in (range(half), range(half, count)):
        for k in panel:
            cols = [lanes(slabs[k], 8 * k + j) for j in range(8)]
            inside = (lane >= 8 * k) & (lane < 8 * k + 8)
            row = jnp.where(lane == sub + 8 * k, 1.0, jnp.where(inside, 0.0, slabs[k]))
            row = pivots(row, cols, sub)
            w = [rows(row, j) for j in range(8)]
            for r in [r for r in panel if r > k] + [r for r in panel if r < k]:
                t0 = jnp.where(inside, 0.0, slabs[r]) - lanes(slabs[r], 8 * k) * w[0]
                t1 = lanes(slabs[r], 8 * k + 1) * w[1]
                for j in range(2, 8, 2):
                    t0 = t0 - lanes(slabs[r], 8 * k + j) * w[j]
                    t1 = t1 + lanes(slabs[r], 8 * k + j + 1) * w[j + 1]
                slabs[r] = t0 - t1
            slabs[k] = row
        start, stop = 8 * panel[0], 8 * panel[-1] + 8
        inside = (lane >= start) & (lane < stop)
        rest = [r for r in range(count) if r not in panel]
        g = jnp.concatenate([slabs[r][:, start:stop] for r in rest], 0)
        change = dot_split(split(g), split(jnp.concatenate([slabs[r] for r in panel], 0)))
        for n, r in enumerate(rest):
            slabs[r] = jnp.where(inside, 0.0, slabs[r]) - change[8 * n : 8 * n + 8]
    return slabs


def row_of(block):
    return jnp.where(block == NB, SHARED, block * BW)


def sweep(front, inverse, wide, block):
    ro = pl.multiple_of(row_of(block), 8)
    co = pl.multiple_of(block * BW, BW)
    out = invert([front[pl.ds(ro + 8 * r, 8), pl.ds(co, BW)] for r in range(BW // 8)])
    for r in range(BW // 8):
        inverse[8 * r : 8 * r + 8, :] = out[r]
    wide[...] = dot_split(split(inverse[...]), split(front[pl.ds(ro, BW), :]))
    wide[:, pl.ds(co, BW)] = inverse[...]
    w = split(wide[...])
    for at, size in [(i * BW, BW) for i in range(NB)] + [(RHS, 8)]:
        g = split(front[at : at + size, pl.ds(co, BW)])
        front[at : at + size, pl.ds(co, BW)] = jnp.zeros((size, BW), jnp.float32)
        front[at : at + size, :] -= dot_split(g, w)


def place(map_ref, row, other):
    mine = [map_ref[row * NB + i] for i in range(NB)]
    theirs = [map_ref[other * NB + i] for i in range(NB)]
    out = []
    for m in mine:
        both = functools.reduce(jnp.logical_or, [m == t for t in theirs])
        out.append(jnp.where(m >= KEEP, m - KEEP, jnp.where(both, NB, -1)))
    return out


def map_rows(tree, level, devices):
    nodes = devices >> level
    node = tree >> level
    return nodes + node - 2, nodes + (node ^ 1) - 2


def write_half(front, pack, half, start):
    for n, (i, j) in enumerate(PAIRS[half * HALF_PAIRS : (half + 1) * HALF_PAIRS]):
        at = start + n * BW
        pack[at : at + BW, :] = front[i * BW : i * BW + BW, j * BW : j * BW + BW]
    for n in range(HALF_RHS):
        at, i = start + HALF_PAIRS * BW + 8 * n, half * HALF_RHS + n
        pack[at : at + 8, :] = front[RHS : RHS + 8, i * BW : i * BW + BW]


def eliminate(front, inverse, wide, flags, blocks, pack, core):
    def step(n, carry):
        @pl.when(flags[n] == 1)
        def _():
            sweep(front, inverse, wide, lax.rem(n + NB, NB + 1))

        return carry

    lax.fori_loop(1 if blocks == NB else 0, NB + 1, step, 0)
    if pack is None:
        return
    if pack.shape[0] == 2 * HALF:
        write_half(front, pack, 0, 0)
        write_half(front, pack, 1, HALF)
        return
    for half in range(2):

        @pl.when(core == half)
        def _():
            write_half(front, pack, half, 0)


def set_flags(flags, map_ref, tree, level, devices):
    if devices >> level == 1:
        for i in range(NB):
            flags[1 + i] = 1
        return
    for i, slot in enumerate(place(map_ref, *map_rows(tree, level, devices))):
        flags[1 + i] = jnp.where(slot < 0, 1, 0)


def leaf_kernel(devices, tree_ref, map_ref, leaf, source, observe, perm, front, pack, inverse, wide, flags):
    front[0:FW, :] = leaf[...]
    eye = lax.broadcasted_iota(jnp.int32, (BW, BW), 0) == lax.broadcasted_iota(jnp.int32, (BW, BW), 1)
    for i in range(NB):
        at = slice(i * BW, i * BW + BW)
        front[at, at] += jnp.where(eye, jnp.broadcast_to(perm[:, at], (BW, BW)), 0.0)
    which = lax.broadcasted_iota(jnp.int32, (8, FW), 0)
    front[RHS : RHS + 8, :] = jnp.where(
        which == 0,
        jnp.broadcast_to(source[...], (8, FW)),
        jnp.where(which == 1, jnp.broadcast_to(observe[...], (8, FW)), 0.0),
    )
    set_flags(flags, map_ref, tree_ref[0], 0, devices)
    eliminate(front, inverse, wide, flags, NB, pack, tree_ref[0] & 1)


def merge_kernel(devices, level, tree_ref, map_ref, own, *rest):
    tree = tree_ref[0]
    if level == 0:
        theirs, rest = rest[0], rest[1:]
    else:
        same, other_half, rest = rest[0], rest[1], rest[2:]
        theirs, rest = rest[-1], rest[:-1]
        core = tree & 1
        theirs[pl.ds(pl.multiple_of(core * HALF, 8), HALF), :] = same[...]
        theirs[pl.ds(pl.multiple_of((1 - core) * HALF, 8), HALF), :] = other_half[...]
    front, rest = rest[0], rest[1:]
    pack = rest[0] if len(rest) == 5 else None
    inverse, wide, flags, slots = rest[-4:]
    row, other = map_rows(tree, level, devices)
    mine, yours = place(map_ref, row, other), place(map_ref, other, row)
    flags[0] = functools.reduce(jnp.maximum, [jnp.where(s == NB, 1, 0) for s in mine])
    set_flags(flags, map_ref, tree, level + 1, devices)
    for i in range(NB):
        slots[i] = mine[i]
    front[...] = jnp.zeros(front.shape, jnp.float32)

    def one(p, carry):
        i, j = p // NB, lax.rem(p, NB)
        a, b = slots[i], slots[j]

        @pl.when((a >= 0) & (b >= 0))
        def _():
            front[pl.ds(pl.multiple_of(row_of(a), 8), BW), pl.ds(pl.multiple_of(b * BW, BW), BW)] = own[
                pl.ds(pl.multiple_of(i * BW, BW), BW), pl.ds(pl.multiple_of(j * BW, BW), BW)
            ]

        return carry

    lax.fori_loop(0, NB * NB, one, 0)
    for i in range(NB):

        @pl.when(mine[i] >= 0)
        def _():
            co = pl.ds(pl.multiple_of(mine[i] * BW, BW), BW)
            front[RHS : RHS + 8, co] = own[RHS : RHS + 8, i * BW : i * BW + BW]

    for p, (i, j) in enumerate(PAIRS):
        a, b = yours[i], yours[j]

        @pl.when((a >= 0) & (b >= 0))
        def _():
            at = p // HALF_PAIRS * HALF + p % HALF_PAIRS * BW
            block = theirs[at : at + BW, :]
            front[pl.ds(pl.multiple_of(row_of(a), 8), BW), pl.ds(pl.multiple_of(b * BW, BW), BW)] += block
            if i != j:
                front[pl.ds(pl.multiple_of(row_of(b), 8), BW), pl.ds(pl.multiple_of(a * BW, BW), BW)] += block.T

    for i in range(NB):

        @pl.when(yours[i] >= 0)
        def _():
            at = i // HALF_RHS * HALF + HALF_PAIRS * BW + i % HALF_RHS * 8
            front[RHS : RHS + 8, pl.ds(pl.multiple_of(yours[i] * BW, BW), BW)] += theirs[at : at + 8, :]

    eliminate(front, inverse, wide, flags, NB + 1, pack, tree & 1)


def recover_kernel(devices, levels, tree_ref, map_ref, *refs):
    fronts, out, kept, solved = refs[: levels + 1], refs[levels + 1], refs[levels + 2], refs[levels + 3]
    tree = tree_ref[0]
    solved[...] = -fronts[levels][RHS : RHS + 8, :]
    for level in reversed(range(levels)):
        front = fronts[level]
        slots = place(map_ref, *map_rows(tree, level, devices))
        for i in range(NB):
            at = slice(i * BW, i * BW + BW)
            kept[:, at] = jnp.zeros((8, BW), jnp.float32)

            @pl.when(slots[i] >= 0)
            def _():
                kept[:, at] = solved[:, pl.ds(pl.multiple_of(slots[i] * BW, BW), BW)]

        width = front.shape[1]
        new = dot_split(split(kept[...]), split(front[0:FW, :])) - front[RHS : RHS + 8, :]
        solved[:, 0:width] = new
        for i in range(NB):
            at = slice(i * BW, i * BW + BW)

            @pl.when(slots[i] >= 0)
            def _():
                solved[:, at] = kept[:, at]

    out[...] = solved[:, 0:FW]


SCALARS = pl.BlockSpec(memory_space=pltpu.SMEM)
WHOLE = pl.BlockSpec(memory_space=pltpu.VMEM)
PARAMS = pltpu.CompilerParams(vmem_limit_bytes=VMEM_LIMIT)


def f32(*shape):
    return jax.ShapeDtypeStruct(shape, jnp.float32)


def scratch(width):
    return [pltpu.VMEM((BW, BW), jnp.float32), pltpu.VMEM((BW, width), jnp.float32), pltpu.SMEM((8,), jnp.int32)]


def leaf_front(devices, tree, maps, leaf, source, observe, perm):
    return pl.pallas_call(
        functools.partial(leaf_kernel, devices),
        out_shape=(f32(SHARED, FW), f32(2 * HALF, BW)),
        in_specs=[SCALARS, SCALARS] + [WHOLE] * 4,
        out_specs=(WHOLE, WHOLE),
        scratch_shapes=scratch(FW),
        compiler_params=PARAMS,
        name="leaf_front",
    )(tree, maps, leaf, source, observe, perm)


def merge(devices, level, tree, maps, own, theirs):
    last = devices >> (level + 1) == 1
    stage = [] if level == 0 else [pltpu.VMEM((2 * HALF, BW), jnp.float32)]
    out = (f32(ROWS, COLS),) + (() if last else (f32(HALF, BW),))
    result = pl.pallas_call(
        functools.partial(merge_kernel, devices, level),
        out_shape=out,
        in_specs=[SCALARS, SCALARS, WHOLE] + [WHOLE] * len(theirs),
        out_specs=(WHOLE,) * len(out),
        scratch_shapes=scratch(COLS) + [pltpu.SMEM((8,), jnp.int32)] + stage,
        compiler_params=PARAMS,
        name=f"merge_{level}",
    )(tree, maps, own, *theirs)
    return result if not last else (result[0], None)


def recover(devices, tree, maps, fronts):
    return pl.pallas_call(
        functools.partial(recover_kernel, devices, len(fronts) - 1),
        out_shape=f32(8, FW),
        in_specs=[SCALARS, SCALARS] + [WHOLE] * len(fronts),
        out_specs=WHOLE,
        scratch_shapes=[pltpu.VMEM((8, FW), jnp.float32), pltpu.VMEM((8, COLS), jnp.float32)],
        compiler_params=PARAMS,
        name="recover",
    )(tree, maps, *fronts)


def partner(block, axis, bit):
    count = lax.axis_size(axis)
    return lax.ppermute(block, axis, [(k, k ^ (1 << bit)) for k in range(count)])


def shards(leaf_matrix, leaf_source, observe, zone_ids, log_perm, block_map):
    leaf_count = lax.axis_size("leaf")
    sub_count = lax.axis_size("sub")
    devices = leaf_count * sub_count
    leaf_bits = leaf_count.bit_length() - 1
    levels = devices.bit_length() - 1
    tree = (lax.axis_index("leaf") + leaf_count * lax.axis_index("sub")).astype(jnp.int32)[None]
    maps = block_map.reshape(-1)
    zones = jnp.broadcast_to(log_perm[None], (devices, log_perm.shape[0]))
    all_zones = lax.all_to_all(zones, ("leaf", "sub"), 0, 0, tiled=True).reshape(-1)
    cells = zone_ids[0]
    perm = jnp.exp(all_zones[cells])
    front, pack = leaf_front(devices, tree, maps, leaf_matrix[0], leaf_source, observe, perm[None])
    fronts = [front]
    for level in range(levels):
        axis, bit = ("leaf", level) if level < leaf_bits else ("sub", level - leaf_bits)
        theirs = (partner(pack, axis, bit),)
        if level > 0:
            theirs += (partner(theirs[0], "leaf", 0),)
        front, pack = merge(devices, level, tree, maps, front, theirs)
        fronts.append(front)
    solution = recover(devices, tree, maps, fronts)
    terms = -perm * solution[0] * solution[1]
    partial = jax.ops.segment_sum(terms, cells, num_segments=all_zones.shape[0])
    shares = lax.all_to_all(partial.reshape(devices, -1), ("leaf", "sub"), 0, 0, tiled=True)
    gradient = shares.sum(0)
    return solution[0][None, :], gradient


def solution(mesh):
    split_all = ("leaf", "sub")
    in_specs = (P(split_all, None, None), P(split_all, None), P(split_all, None), P(split_all, None), P(split_all), P())
    out_specs = (P(split_all, None), P(split_all))
    return jax.shard_map(shards, mesh=mesh, in_specs=in_specs, out_specs=out_specs, check_vma=False)
```

```python
import functools

import jax
import jax.numpy as jnp
from jax import lax
from jax.experimental import pallas as pl
from jax.experimental.pallas import tpu as pltpu
from jax.sharding import PartitionSpec as P

BW = 128
NB = 4
KEEP = NB - 1
FW = NB * BW
NEVER = 99
STRIDE = 16
VMEM_LIMIT = 48 * 1024 * 1024


def split(x):
    high = x.astype(jnp.bfloat16)
    return high, (x - high.astype(jnp.float32)).astype(jnp.bfloat16)


def dot_split(a, b):
    one = functools.partial(jnp.dot, preferred_element_type=jnp.float32)
    both = one(jnp.concatenate([a[0], a[1]], 1), jnp.concatenate([b[0], b[0]], 0))
    return both + one(a[0], b[1])


def dot_split_left(a, b):
    one = functools.partial(
        lax.dot_general, dimension_numbers=(((0,), (0,)), ((), ())), preferred_element_type=jnp.float32
    )
    both = one(jnp.concatenate([a[0], a[1]], 0), jnp.concatenate([b[0], b[0]], 0))
    return both + one(a[0], b[1])


def dot_split_right(a, b):
    one = functools.partial(
        lax.dot_general, dimension_numbers=(((1,), (1,)), ((), ())), preferred_element_type=jnp.float32
    )
    both = one(jnp.concatenate([a[0], a[1]], 1), jnp.concatenate([b[0], b[0]], 1))
    return both + one(a[0], b[1])


def lanes(x, c):
    return jnp.broadcast_to(x[:, c : c + 1], (8, BW))


def rows(x, j):
    return jnp.broadcast_to(x[j : j + 1, :], (8, BW))


def pivots(row, cols, sub):
    for j in range(0, 8, 2):
        left, right = cols[j], cols[j + 1]
        a, b, c = rows(left, j), rows(left, j + 1), rows(right, j + 1)
        scale = 1.0 / (a * c - b * b)
        first, second = sub == j, sub == j + 1

        def update(v):
            v0, v1 = rows(v, j), rows(v, j + 1)
            u0 = c * v0 - b * v1
            u1 = a * v1 - b * v0
            t = left * u0 + right * u1
            return jnp.where(first, u0 * scale, jnp.where(second, u1 * scale, v - t * scale))

        row = update(row)
        for m in range(j + 2, 8):
            cols[m] = update(cols[m])
    return row


def invert(slabs):
    lane = lax.broadcasted_iota(jnp.int32, (8, BW), 1)
    sub = lax.broadcasted_iota(jnp.int32, (8, BW), 0)
    slabs = list(slabs)
    count = len(slabs)
    half = count // 2
    for panel in (range(half), range(half, count)):
        for k in panel:
            cols = [lanes(slabs[k], 8 * k + j) for j in range(8)]
            inside = (lane >= 8 * k) & (lane < 8 * k + 8)
            row = jnp.where(lane == sub + 8 * k, 1.0, jnp.where(inside, 0.0, slabs[k]))
            row = pivots(row, cols, sub)
            w = [rows(row, j) for j in range(8)]
            for r in [r for r in panel if r > k] + [r for r in panel if r < k]:
                t0 = jnp.where(inside, 0.0, slabs[r]) - lanes(slabs[r], 8 * k) * w[0]
                t1 = lanes(slabs[r], 8 * k + 1) * w[1]
                for j in range(2, 8, 2):
                    t0 = t0 - lanes(slabs[r], 8 * k + j) * w[j]
                    t1 = t1 + lanes(slabs[r], 8 * k + j + 1) * w[j + 1]
                slabs[r] = t0 - t1
            slabs[k] = row
        start, stop = 8 * panel[0], 8 * panel[-1] + 8
        inside = (lane >= start) & (lane < stop)
        rest = [r for r in range(count) if r not in panel]
        g = jnp.concatenate([slabs[r][:, start:stop] for r in rest], 0)
        change = dot_split(split(g), split(jnp.concatenate([slabs[r] for r in panel], 0)))
        for n, r in enumerate(rest):
            slabs[r] = jnp.where(inside, 0.0, slabs[r]) - change[8 * n : 8 * n + 8]
    return slabs


def span(block):
    return pl.ds(pl.multiple_of(block * BW, BW), BW)


def invert_ref(load, store):
    out = invert([load(8 * r) for r in range(BW // 8)])
    for r in range(BW // 8):
        store[8 * r : 8 * r + 8, :] = out[r]


def sweep(front, inverse, wide, block):
    at = pl.multiple_of(block * BW, BW)
    invert_ref(lambda r: front[pl.ds(at + r, 8), pl.ds(at, BW)], inverse)
    wide[...] = dot_split(split(inverse[...]), split(front[pl.ds(at, BW), :]))
    wide[:, pl.ds(at, BW)] = inverse[...]
    w = split(wide[...])
    for start, size in [(i * BW, BW) for i in range(NB)] + [(FW, 8)]:
        g = split(front[start : start + size, pl.ds(at, BW)])
        front[start : start + size, pl.ds(at, BW)] = jnp.zeros((size, BW), jnp.float32)
        front[start : start + size, :] -= dot_split(g, w)


def active(levels, level):
    return min(NB, levels - level)


def pairs(count):
    return [(a, b) for a in range(count) for b in range(a, count)]


def parts(count):
    return 1 if count * (count + 1) // 2 % 2 else 2


def part_rows(count):
    return len(pairs(count)) // parts(count) * BW + -(-count // parts(count)) * 8


def block_row(count, p):
    each = len(pairs(count)) // parts(count)
    return p // each * part_rows(count) + p % each * BW


def rhs_row(count, a):
    each = -(-count // parts(count))
    return a // each * part_rows(count) + len(pairs(count)) // parts(count) * BW + a % each * 8


def write_pack(front, pack, count, core, at, rhs, valid):
    size = part_rows(count)
    whole = pack.shape[0] == parts(count) * size

    def put(start, height, source, ok):
        part = start // size
        to = start if whole else start % size
        ok = ok if whole else ok & (core == part)

        @pl.when(ok)
        def _():
            pack[to : to + height, :] = source()

    for p, (a, b) in enumerate(pairs(count)):
        put(block_row(count, p), BW, lambda a=a, b=b: front[at(a), at(b)], valid(a) & valid(b))
    for a in range(count):
        put(rhs_row(count, a), 8, lambda a=a: front[rhs : rhs + 8, at(a)], valid(a))


def plan_kernel(levels, tree_ref, map_ref, plan, when, position):
    tree = tree_ref[0]
    for i in range(NB):
        when[levels * NB + i] = NEVER
        position[levels * NB + i] = -1
    for level in reversed(range(levels)):
        nodes, node = (1 << levels) >> level, tree >> level
        mine, yours = (
            [map_ref[(nodes + n - 2) * NB + i] for i in range(NB)] for n in (node, node ^ 1)
        )
        dropped = active(levels, level + 1)
        for child, other, base in ((mine, yours, 0), (yours, mine, 4)):
            after, spot, place = [], [], []
            for m in child:
                both = functools.reduce(jnp.logical_or, [m == o for o in other])
                above = (level + 1) * NB + jnp.maximum(m - KEEP, 0)
                later = jnp.where(m >= KEEP, when[above], NEVER)
                after.append(jnp.where(both, level, later))
                place.append(jnp.where(later < NEVER, position[above], jnp.where(both, dropped, -1)))
            for i in range(NB):
                ahead = functools.reduce(jnp.add, [jnp.where(after[k] < after[i], 1, 0) for k in range(NB) if k != i])
                spot.append(jnp.where(after[i] < NEVER, ahead, -1))
            for a in range(NB):
                slot, order = jnp.int32(-1), jnp.int32(-1)
                for i in range(NB):
                    slot = jnp.where(spot[i] == a, place[i], slot)
                    order = jnp.where(spot[i] == a, i, order)
                plan[level * STRIDE + base + a] = slot
                if level == 0 and base == 0:
                    plan[levels * STRIDE + a] = order
            if base == 0:
                for i in range(NB):
                    when[level * NB + i] = after[i]
                    position[level * NB + i] = spot[i]
                    if level == 0:
                        plan[levels * STRIDE + 4 + i] = spot[i]
        plan[level * STRIDE + 8] = jnp.where(plan[level * STRIDE] == dropped, 1, 0)


def leaf_kernel(levels, plan, leaf, source, observe, perm, front, pack, inverse, wide):
    front[0:FW, :] = leaf[...]
    eye = lax.broadcasted_iota(jnp.int32, (BW, BW), 0) == lax.broadcasted_iota(jnp.int32, (BW, BW), 1)
    for i in range(NB):
        at = slice(i * BW, i * BW + BW)
        front[at, at] += jnp.where(eye, jnp.broadcast_to(perm[:, at], (BW, BW)), 0.0)
    which = lax.broadcasted_iota(jnp.int32, (8, FW), 0)
    front[FW : FW + 8, :] = jnp.where(
        which == 0,
        jnp.broadcast_to(source[...], (8, FW)),
        jnp.where(which == 1, jnp.broadcast_to(observe[...], (8, FW)), 0.0),
    )
    order = [plan[levels * STRIDE + a] for a in range(NB)]

    def step(i, carry):
        @pl.when(plan[levels * STRIDE + 4 + i] < 0)
        def _():
            sweep(front, inverse, wide, i)

        return carry

    lax.fori_loop(0, NB, step, 0)
    count = active(levels, 0)
    write_pack(
        front, pack, count, 0, lambda a: span(jnp.maximum(order[a], 0)), FW, lambda a: order[a] >= 0
    )


def merge_kernel(levels, level, core_ref, plan, own, *rest):
    below, count = active(levels, level), active(levels, level + 1)
    core = core_ref[0]
    base = level * STRIDE
    if level > 0 and parts(below) == 2:
        same, swapped, *rest, theirs = rest
        size = part_rows(below)
        theirs[pl.ds(pl.multiple_of(core * size, 8), size), :] = same[...]
        theirs[pl.ds(pl.multiple_of((1 - core) * size, 8), size), :] = swapped[...]
    else:
        theirs, *rest = rest
    if count:
        coupling, reduced, front, pack, diagonal, inverse, coupled = rest
        front[...] = jnp.zeros(front.shape, jnp.float32)
        coupled[...] = jnp.zeros(coupled.shape, jnp.float32)
    else:
        reduced, diagonal, inverse = rest
    mine = [plan[base + a] for a in range(below)]
    yours = [plan[base + 4 + a] for a in range(below)]
    eliminated = plan[base + 8] == 1
    kept = plan[base + 8] == 0
    rhs = count * BW
    if level == 0:
        order = [jnp.maximum(plan[levels * STRIDE + a], 0) for a in range(below)]
        at, own_rhs = lambda a: span(order[a]), FW
    else:
        at, own_rhs = lambda a: slice(a * BW, a * BW + BW), below * BW
    their_rows = {p: block_row(below, n) for n, p in enumerate(pairs(below))}
    their_block = lambda a, b: theirs[their_rows[a, b] : their_rows[a, b] + BW, :]
    their_rhs = lambda a: theirs[rhs_row(below, a) : rhs_row(below, a) + 8, :]
    diagonal[...] = own[at(0), at(0)] + their_block(0, 0)
    right = own[own_rhs : own_rhs + 8, at(0)] + their_rhs(0)
    reduced[...] = right

    def put(ok, a, b, value):
        @pl.when(ok)
        def _():
            front[span(a), span(b)] = value()

    def put_rhs(ok, a, value):
        @pl.when(ok)
        def _():
            front[rhs : rhs + 8, span(a)] = value()

    if count:
        put(kept, mine[0], mine[0], lambda: diagonal[...])
        put_rhs(kept, mine[0], lambda: reduced[...])
        for a in range(1, below):
            for slots, block, across, vector in (
                (mine, lambda a, b: own[at(a), at(b)], lambda a, b: own[at(b), at(a)], lambda a: own[own_rhs : own_rhs + 8, at(a)]),
                (yours, their_block, lambda a, b: their_block(a, b).T, their_rhs),
            ):
                there = slots[a] >= 0

                @pl.when(there & eliminated)
                def _():
                    coupled[:, span(slots[a])] = block(0, a)

                put(there & kept, slots[0], slots[a], lambda: block(0, a))
                put(there & kept, slots[a], slots[0], lambda: across(0, a))
                put_rhs(there, slots[a], lambda: vector(a))
                for b in range(a, below):
                    both = there & (slots[b] >= 0)
                    put(both, slots[a], slots[b], lambda: block(a, b))
                    if a != b:
                        put(both, slots[b], slots[a], lambda: across(a, b))

    @pl.when(eliminated)
    def _():
        invert_ref(lambda r: diagonal[r : r + 8, :], inverse)
        d, r = split(inverse[...]), split(reduced[...])
        if count:
            c = split(coupled[...])
            w = dot_split(d, c)
            coupling[...] = w
            w = split(w)
            front[0:rhs, :] -= dot_split_left(c, w)
            front[rhs : rhs + 8, :] -= dot_split(r, w)
        reduced[...] = dot_split(r, d)

    if count:

        @pl.when(kept)
        def _():
            coupling[...] = jnp.zeros(coupling.shape, jnp.float32)

        write_pack(
            front, pack, count, core, lambda a: slice(a * BW, a * BW + BW), rhs, lambda a: plan[0] == plan[0]
        )


def pick(blocks, slot):
    out = jnp.zeros((8, BW), jnp.float32)
    for n, block in enumerate(blocks):
        out = jnp.where(slot == n, block, out)
    return out


def recover_kernel(levels, plan, *refs):
    couplings, reduced = refs[: levels - 1], refs[levels - 1 : 2 * levels - 1]
    leaf, out = refs[2 * levels - 1 :]
    solved = [reduced[levels - 1][...]]
    for level in reversed(range(1, levels)):
        kept = [pick(solved, plan[level * STRIDE + a]) for a in range(active(levels, level))]
        z = split(jnp.concatenate(kept, 1))
        solved = kept + [reduced[level - 1][...] - dot_split_right(z, split(couplings[level - 1][...]))]
    spots = [plan[levels * STRIDE + 4 + i] for i in range(NB)]
    kept = [pick(solved, jnp.where(spot >= 0, plan[jnp.maximum(spot, 0)], -1)) for spot in spots]
    new = dot_split(split(jnp.concatenate(kept, 1)), split(leaf[0:FW, :])) - leaf[FW : FW + 8, :]
    for i in range(NB):
        at = slice(i * BW, i * BW + BW)
        out[:, at] = jnp.where(spots[i] >= 0, kept[i], new[:, at])


SCALARS = pl.BlockSpec(memory_space=pltpu.SMEM)
WHOLE = pl.BlockSpec(memory_space=pltpu.VMEM)
PARAMS = pltpu.CompilerParams(vmem_limit_bytes=VMEM_LIMIT)


def f32(*shape):
    return jax.ShapeDtypeStruct(shape, jnp.float32)


def vmem(*shape):
    return pltpu.VMEM(shape, jnp.float32)


def make_plan(levels, tree, maps):
    return pl.pallas_call(
        functools.partial(plan_kernel, levels),
        out_shape=jax.ShapeDtypeStruct(((levels + 1) * STRIDE,), jnp.int32),
        in_specs=[SCALARS, SCALARS],
        out_specs=SCALARS,
        scratch_shapes=[pltpu.SMEM(((levels + 1) * NB,), jnp.int32)] * 2,
        name="make_plan",
    )(tree, maps)


def leaf_front(levels, plan, leaf, source, observe, perm):
    count = active(levels, 0)
    return pl.pallas_call(
        functools.partial(leaf_kernel, levels),
        out_shape=(f32(FW + 8, FW), f32(parts(count) * part_rows(count), BW)),
        in_specs=[SCALARS] + [WHOLE] * 4,
        out_specs=(WHOLE, WHOLE),
        scratch_shapes=[vmem(BW, BW), vmem(BW, FW)],
        compiler_params=PARAMS,
        name="leaf_front",
    )(plan, leaf, source, observe, perm)


def merge(levels, level, core, plan, own, theirs):
    below, count = active(levels, level), active(levels, level + 1)
    n = count * BW
    out, work = (f32(8, BW),), [vmem(BW, BW), vmem(BW, BW)]
    if count:
        out = (f32(BW, n),) + out + (f32(n + 8, n), f32(part_rows(count), BW))
        work += [vmem(BW, n)]
    if len(theirs) == 2:
        work += [vmem(2 * part_rows(below), BW)]
    return pl.pallas_call(
        functools.partial(merge_kernel, levels, level),
        out_shape=out,
        in_specs=[SCALARS, SCALARS, WHOLE] + [WHOLE] * len(theirs),
        out_specs=(WHOLE,) * len(out),
        scratch_shapes=work,
        compiler_params=PARAMS,
        name=f"merge_{level}",
    )(core, plan, own, *theirs)


def recover(levels, plan, couplings, reduced, leaf):
    return pl.pallas_call(
        functools.partial(recover_kernel, levels),
        out_shape=f32(8, FW),
        in_specs=[SCALARS] + [WHOLE] * (2 * levels),
        out_specs=WHOLE,
        compiler_params=PARAMS,
        name="recover",
    )(plan, *couplings, *reduced, leaf)


def partner(block, axis, bit):
    count = lax.axis_size(axis)
    return lax.ppermute(block, axis, [(k, k ^ (1 << bit)) for k in range(count)])


def shards(leaf_matrix, leaf_source, observe, zone_ids, log_perm, block_map):
    leaf_count = lax.axis_size("leaf")
    devices = leaf_count * lax.axis_size("sub")
    leaf_bits = leaf_count.bit_length() - 1
    levels = devices.bit_length() - 1
    tree = (lax.axis_index("leaf") + leaf_count * lax.axis_index("sub")).astype(jnp.int32)[None]
    core = tree & 1
    plan = make_plan(levels, tree, block_map.reshape(-1))
    zones = jnp.broadcast_to(log_perm[None], (devices, log_perm.shape[0]))
    all_zones = lax.all_to_all(zones, ("leaf", "sub"), 0, 0, tiled=True).reshape(-1)
    cells = zone_ids[0]
    perm = jnp.exp(all_zones[cells])
    leaf, pack = leaf_front(levels, plan, leaf_matrix[0], leaf_source, observe, perm[None])
    front, couplings, reduced = leaf, [], []
    for level in range(levels):
        axis, bit = ("leaf", level) if level < leaf_bits else ("sub", level - leaf_bits)
        theirs = (partner(pack, axis, bit),)
        if level > 0 and parts(active(levels, level)) == 2:
            theirs += (partner(theirs[0], "leaf", 0),)
        *more, front, pack = merge(levels, level, core, plan, front, theirs) + ((None, None) if level == levels - 1 else ())
        couplings += more[:-1]
        reduced += more[-1:]
    solution = recover(levels, plan, couplings, reduced, leaf)
    terms = -perm * solution[0] * solution[1]
    partial = jax.ops.segment_sum(terms, cells, num_segments=all_zones.shape[0])
    shares = lax.all_to_all(partial.reshape(devices, -1), ("leaf", "sub"), 0, 0, tiled=True)
    return solution[0][None, :], shares.sum(0)


def solution(mesh):
    split_all = ("leaf", "sub")
    in_specs = (P(split_all, None, None), P(split_all, None), P(split_all, None), P(split_all, None), P(split_all), P())
    out_specs = (P(split_all, None), P(split_all))
    return jax.shard_map(shards, mesh=mesh, in_specs=in_specs, out_specs=out_specs, check_vma=False)
```

```python
import functools

import jax
import jax.numpy as jnp
from jax import lax
from jax.experimental import pallas as pl
from jax.experimental.pallas import tpu as pltpu
from jax.sharding import PartitionSpec as P

BW = 128
NB = 4
KEEP = NB - 1
FW = NB * BW
SLOTS = 64
NEVER = 99
STRIDE = 16
VMEM_LIMIT = 48 * 1024 * 1024


def split(x):
    high = x.astype(jnp.bfloat16)
    return high, (x - high.astype(jnp.float32)).astype(jnp.bfloat16)


def dot_split(a, b):
    one = functools.partial(jnp.dot, preferred_element_type=jnp.float32)
    both = one(jnp.concatenate([a[0], a[1]], 1), jnp.concatenate([b[0], b[0]], 0))
    return both + one(a[0], b[1])


def dot_split_left(a, b):
    one = functools.partial(
        lax.dot_general, dimension_numbers=(((0,), (0,)), ((), ())), preferred_element_type=jnp.float32
    )
    both = one(jnp.concatenate([a[0], a[1]], 0), jnp.concatenate([b[0], b[0]], 0))
    return both + one(a[0], b[1])


def dot_split_right(a, b):
    one = functools.partial(
        lax.dot_general, dimension_numbers=(((1,), (1,)), ((), ())), preferred_element_type=jnp.float32
    )
    both = one(jnp.concatenate([a[0], a[1]], 1), jnp.concatenate([b[0], b[0]], 1))
    return both + one(a[0], b[1])


def lanes(x, c):
    return jnp.broadcast_to(x[:, c : c + 1], (8, BW))


def rows(x, j):
    return jnp.broadcast_to(x[j : j + 1, :], (8, BW))


def pivots(row, cols, sub, buffer, slot):
    def pair(v, j):
        slot[0] = (slot[0] + 1) % SLOTS
        at = 8 * slot[0]
        buffer[at : at + 8, :] = v
        return [jnp.broadcast_to(buffer[at + i : at + i + 1, :], (8, BW)) for i in (j, j + 1)]

    for j in range(0, 8, 2):
        left, right = cols[j], cols[j + 1]
        spread = {m: pair(cols[m], j) for m in range(j, 8)}
        a, b, c = spread[j][0], spread[j][1], spread[j + 1][1]
        scale = 1.0 / (a * c - b * b)
        first, second = sub == j, sub == j + 1

        def update(v, v0, v1):
            u0 = c * v0 - b * v1
            u1 = a * v1 - b * v0
            t = left * u0 + right * u1
            return jnp.where(first, u0 * scale, jnp.where(second, u1 * scale, v - t * scale))

        row = update(row, *pair(row, j))
        for m in range(j + 2, 8):
            cols[m] = update(cols[m], *spread[m])
    return row


def invert(slabs, buffer):
    lane = lax.broadcasted_iota(jnp.int32, (8, BW), 1)
    sub = lax.broadcasted_iota(jnp.int32, (8, BW), 0)
    slabs = list(slabs)
    count = len(slabs)
    half = count // 2
    slot = [0]
    for panel in (range(half), range(half, count)):
        for k in panel:
            cols = [lanes(slabs[k], 8 * k + j) for j in range(8)]
            inside = (lane >= 8 * k) & (lane < 8 * k + 8)
            row = jnp.where(lane == sub + 8 * k, 1.0, jnp.where(inside, 0.0, slabs[k]))
            row = pivots(row, cols, sub, buffer, slot)
            w = [rows(row, j) for j in range(8)]
            for r in [r for r in panel if r > k] + [r for r in panel if r < k]:
                t0 = jnp.where(inside, 0.0, slabs[r]) - lanes(slabs[r], 8 * k) * w[0]
                t1 = lanes(slabs[r], 8 * k + 1) * w[1]
                for j in range(2, 8, 2):
                    t0 = t0 - lanes(slabs[r], 8 * k + j) * w[j]
                    t1 = t1 + lanes(slabs[r], 8 * k + j + 1) * w[j + 1]
                slabs[r] = t0 - t1
            slabs[k] = row
        start, stop = 8 * panel[0], 8 * panel[-1] + 8
        inside = (lane >= start) & (lane < stop)
        rest = [r for r in range(count) if r not in panel]
        g = jnp.concatenate([slabs[r][:, start:stop] for r in rest], 0)
        change = dot_split(split(g), split(jnp.concatenate([slabs[r] for r in panel], 0)))
        for n, r in enumerate(rest):
            slabs[r] = jnp.where(inside, 0.0, slabs[r]) - change[8 * n : 8 * n + 8]
    return slabs


def span(block):
    return pl.ds(pl.multiple_of(block * BW, BW), BW)


def invert_ref(load, store, buffer):
    out = invert([load(8 * r) for r in range(BW // 8)], buffer)
    for r in range(BW // 8):
        store[8 * r : 8 * r + 8, :] = out[r]


def sweep(front, inverse, wide, buffer, block):
    at = pl.multiple_of(block * BW, BW)
    invert_ref(lambda r: front[pl.ds(at + r, 8), pl.ds(at, BW)], inverse, buffer)
    wide[...] = dot_split(split(inverse[...]), split(front[pl.ds(at, BW), :]))
    wide[:, pl.ds(at, BW)] = inverse[...]
    w = split(wide[...])
    for start, size in [(i * BW, BW) for i in range(NB)] + [(FW, 8)]:
        g = split(front[start : start + size, pl.ds(at, BW)])
        front[start : start + size, pl.ds(at, BW)] = jnp.zeros((size, BW), jnp.float32)
        front[start : start + size, :] -= dot_split(g, w)


def active(levels, level):
    return min(NB, levels - level)


def pairs(count):
    return [(a, b) for a in range(count) for b in range(a, count)]


def parts(count):
    return 1 if count * (count + 1) // 2 % 2 else 2


def part_rows(count):
    return len(pairs(count)) // parts(count) * BW + -(-count // parts(count)) * 8


def block_row(count, p):
    each = len(pairs(count)) // parts(count)
    return p // each * part_rows(count) + p % each * BW


def rhs_row(count, a):
    each = -(-count // parts(count))
    return a // each * part_rows(count) + len(pairs(count)) // parts(count) * BW + a % each * 8


def write_pack(front, pack, count, core, at, rhs, valid):
    size = part_rows(count)
    whole = pack.shape[0] == parts(count) * size

    def put(start, height, source, ok):
        part = start // size
        to = start if whole else start % size
        ok = ok if whole else ok & (core == part)

        @pl.when(ok)
        def _():
            pack[to : to + height, :] = source()

    for p, (a, b) in enumerate(pairs(count)):
        put(block_row(count, p), BW, lambda a=a, b=b: front[at(a), at(b)], valid(a) & valid(b))
    for a in range(count):
        put(rhs_row(count, a), 8, lambda a=a: front[rhs : rhs + 8, at(a)], valid(a))


def plan_kernel(levels, tree_ref, map_ref, plan, when, position):
    tree = tree_ref[0]
    for i in range(NB):
        when[levels * NB + i] = NEVER
        position[levels * NB + i] = -1
    for level in reversed(range(levels)):
        nodes, node = (1 << levels) >> level, tree >> level
        mine, yours = (
            [map_ref[(nodes + n - 2) * NB + i] for i in range(NB)] for n in (node, node ^ 1)
        )
        dropped = active(levels, level + 1)
        for child, other, base in ((mine, yours, 0), (yours, mine, 4)):
            after, spot, place = [], [], []
            for m in child:
                both = functools.reduce(jnp.logical_or, [m == o for o in other])
                above = (level + 1) * NB + jnp.maximum(m - KEEP, 0)
                later = jnp.where(m >= KEEP, when[above], NEVER)
                after.append(jnp.where(both, level, later))
                place.append(jnp.where(later < NEVER, position[above], jnp.where(both, dropped, -1)))
            for i in range(NB):
                ahead = functools.reduce(jnp.add, [jnp.where(after[k] < after[i], 1, 0) for k in range(NB) if k != i])
                spot.append(jnp.where(after[i] < NEVER, ahead, -1))
            for a in range(NB):
                slot, order = jnp.int32(-1), jnp.int32(-1)
                for i in range(NB):
                    slot = jnp.where(spot[i] == a, place[i], slot)
                    order = jnp.where(spot[i] == a, i, order)
                plan[level * STRIDE + base + a] = slot
                if level == 0 and base == 0:
                    plan[levels * STRIDE + a] = order
            if base == 0:
                for i in range(NB):
                    when[level * NB + i] = after[i]
                    position[level * NB + i] = spot[i]
                    if level == 0:
                        plan[levels * STRIDE + 4 + i] = spot[i]
        plan[level * STRIDE + 8] = jnp.where(plan[level * STRIDE] == dropped, 1, 0)


def leaf_kernel(levels, plan, leaf, source, observe, perm, front, pack, inverse, wide, buffer):
    front[0:FW, :] = leaf[...]
    eye = lax.broadcasted_iota(jnp.int32, (BW, BW), 0) == lax.broadcasted_iota(jnp.int32, (BW, BW), 1)
    for i in range(NB):
        at = slice(i * BW, i * BW + BW)
        front[at, at] += jnp.where(eye, jnp.broadcast_to(perm[:, at], (BW, BW)), 0.0)
    which = lax.broadcasted_iota(jnp.int32, (8, FW), 0)
    front[FW : FW + 8, :] = jnp.where(
        which == 0,
        jnp.broadcast_to(source[...], (8, FW)),
        jnp.where(which == 1, jnp.broadcast_to(observe[...], (8, FW)), 0.0),
    )
    order = [plan[levels * STRIDE + a] for a in range(NB)]

    def step(i, carry):
        @pl.when(plan[levels * STRIDE + 4 + i] < 0)
        def _():
            sweep(front, inverse, wide, buffer, i)

        return carry

    lax.fori_loop(0, NB, step, 0)
    count = active(levels, 0)
    write_pack(
        front, pack, count, 0, lambda a: span(jnp.maximum(order[a], 0)), FW, lambda a: order[a] >= 0
    )


def inverse_kernel(level, plan, own, theirs, inverse, buffer):
    @pl.when(plan[level * STRIDE + 8] == 1)
    def _():
        inverse[...] = own[...] + theirs[...]
        invert_ref(lambda r: inverse[r : r + 8, :], inverse, buffer)


def early(levels, level):
    return 0 < level < levels - 1


def merge_kernel(levels, level, core_ref, plan, own, *rest):
    if early(levels, level):
        ahead, *rest = rest
    below, count = active(levels, level), active(levels, level + 1)
    core = core_ref[0]
    base = level * STRIDE
    if level > 0 and parts(below) == 2:
        same, swapped, *rest, theirs = rest
        size = part_rows(below)
        theirs[pl.ds(pl.multiple_of(core * size, 8), size), :] = same[...]
        theirs[pl.ds(pl.multiple_of((1 - core) * size, 8), size), :] = swapped[...]
    else:
        theirs, *rest = rest
    if not early(levels, level):
        *rest, ahead, buffer = rest
    if early(levels, level + 1):
        lead, *rest = rest
    if count:
        coupling, reduced, front, pack, diagonal, coupled = rest
        front[...] = jnp.zeros(front.shape, jnp.float32)
        coupled[...] = jnp.zeros(coupled.shape, jnp.float32)
    else:
        reduced, diagonal = rest
    mine = [plan[base + a] for a in range(below)]
    yours = [plan[base + 4 + a] for a in range(below)]
    eliminated = plan[base + 8] == 1
    kept = plan[base + 8] == 0
    rhs = count * BW
    if level == 0:
        order = [jnp.maximum(plan[levels * STRIDE + a], 0) for a in range(below)]
        at, own_rhs = lambda a: span(order[a]), FW
    else:
        at, own_rhs = lambda a: slice(a * BW, a * BW + BW), below * BW
    their_rows = {p: block_row(below, n) for n, p in enumerate(pairs(below))}
    their_block = lambda a, b: theirs[their_rows[a, b] : their_rows[a, b] + BW, :]
    their_rhs = lambda a: theirs[rhs_row(below, a) : rhs_row(below, a) + 8, :]
    diagonal[...] = own[at(0), at(0)] + their_block(0, 0)
    right = own[own_rhs : own_rhs + 8, at(0)] + their_rhs(0)
    reduced[...] = right

    def put(ok, a, b, value):
        @pl.when(ok)
        def _():
            front[span(a), span(b)] = value()

    def put_rhs(ok, a, value):
        @pl.when(ok)
        def _():
            front[rhs : rhs + 8, span(a)] = value()

    if count:
        put(kept, mine[0], mine[0], lambda: diagonal[...])
        put_rhs(kept, mine[0], lambda: reduced[...])
        for a in range(1, below):
            for slots, block, across, vector in (
                (mine, lambda a, b: own[at(a), at(b)], lambda a, b: own[at(b), at(a)], lambda a: own[own_rhs : own_rhs + 8, at(a)]),
                (yours, their_block, lambda a, b: their_block(a, b).T, their_rhs),
            ):
                there = slots[a] >= 0

                @pl.when(there & eliminated)
                def _():
                    coupled[:, span(slots[a])] = block(0, a)

                put(there & kept, slots[0], slots[a], lambda: block(0, a))
                put(there & kept, slots[a], slots[0], lambda: across(0, a))
                put_rhs(there, slots[a], lambda: vector(a))
                for b in range(a, below):
                    both = there & (slots[b] >= 0)
                    put(both, slots[a], slots[b], lambda: block(a, b))
                    if a != b:
                        put(both, slots[b], slots[a], lambda: across(a, b))

    @pl.when(eliminated)
    def _():
        if not early(levels, level):
            invert_ref(lambda r: diagonal[r : r + 8, :], ahead, buffer)
        d, r = split(ahead[...]), split(reduced[...])
        if count:
            c = split(coupled[...])
            w = dot_split(d, c)
            coupling[...] = w
            w = split(w)
            front[0:rhs, :] -= dot_split_left(c, w)
            front[rhs : rhs + 8, :] -= dot_split(r, w)
        reduced[...] = dot_split(r, d)

    if count:

        @pl.when(kept)
        def _():
            coupling[...] = jnp.zeros(coupling.shape, jnp.float32)

        write_pack(
            front, pack, count, core, lambda a: slice(a * BW, a * BW + BW), rhs, lambda a: plan[0] == plan[0]
        )
        if early(levels, level + 1):
            lead[...] = front[0:BW, 0:BW]


def pick(blocks, slot):
    out = jnp.zeros((8, BW), jnp.float32)
    for n, block in enumerate(blocks):
        out = jnp.where(slot == n, block, out)
    return out


def recover_kernel(levels, plan, *refs):
    couplings, reduced = refs[: levels - 1], refs[levels - 1 : 2 * levels - 1]
    leaf, out = refs[2 * levels - 1 :]
    solved = [reduced[levels - 1][...]]
    for level in reversed(range(1, levels)):
        kept = [pick(solved, plan[level * STRIDE + a]) for a in range(active(levels, level))]
        z = split(jnp.concatenate(kept, 1))
        solved = kept + [reduced[level - 1][...] - dot_split_right(z, split(couplings[level - 1][...]))]
    spots = [plan[levels * STRIDE + 4 + i] for i in range(NB)]
    kept = [pick(solved, jnp.where(spot >= 0, plan[jnp.maximum(spot, 0)], -1)) for spot in spots]
    new = dot_split(split(jnp.concatenate(kept, 1)), split(leaf[0:FW, :])) - leaf[FW : FW + 8, :]
    for i in range(NB):
        at = slice(i * BW, i * BW + BW)
        out[:, at] = jnp.where(spots[i] >= 0, kept[i], new[:, at])


SCALARS = pl.BlockSpec(memory_space=pltpu.SMEM)
WHOLE = pl.BlockSpec(memory_space=pltpu.VMEM)
PARAMS = pltpu.CompilerParams(vmem_limit_bytes=VMEM_LIMIT)


def f32(*shape):
    return jax.ShapeDtypeStruct(shape, jnp.float32)


def vmem(*shape):
    return pltpu.VMEM(shape, jnp.float32)


def make_plan(levels, tree, maps):
    return pl.pallas_call(
        functools.partial(plan_kernel, levels),
        out_shape=jax.ShapeDtypeStruct(((levels + 1) * STRIDE,), jnp.int32),
        in_specs=[SCALARS, SCALARS],
        out_specs=SCALARS,
        scratch_shapes=[pltpu.SMEM(((levels + 1) * NB,), jnp.int32)] * 2,
        name="make_plan",
    )(tree, maps)


def leaf_front(levels, plan, leaf, source, observe, perm):
    count = active(levels, 0)
    return pl.pallas_call(
        functools.partial(leaf_kernel, levels),
        out_shape=(f32(FW + 8, FW), f32(parts(count) * part_rows(count), BW)),
        in_specs=[SCALARS] + [WHOLE] * 4,
        out_specs=(WHOLE, WHOLE),
        scratch_shapes=[vmem(BW, BW), vmem(BW, FW), vmem(8 * SLOTS, BW)],
        compiler_params=PARAMS,
        name="leaf_front",
    )(plan, leaf, source, observe, perm)


def shared_inverse(level, plan, own, theirs):
    return pl.pallas_call(
        functools.partial(inverse_kernel, level),
        out_shape=f32(BW, BW),
        in_specs=[SCALARS, WHOLE, WHOLE],
        out_specs=WHOLE,
        scratch_shapes=[vmem(8 * SLOTS, BW)],
        compiler_params=PARAMS,
        cost_estimate=pl.CostEstimate(flops=4 * BW**3, bytes_accessed=12 * BW * BW, transcendentals=0),
        name=f"inverse_{level}",
    )(plan, own, theirs)


def merge(levels, level, core, plan, own, theirs, ahead):
    below, count = active(levels, level), active(levels, level + 1)
    n = count * BW
    out, work = (f32(8, BW),), [vmem(BW, BW)]
    if count:
        out = (f32(BW, n),) + out + (f32(n + 8, n), f32(part_rows(count), BW))
        work += [vmem(BW, n)]
    if early(levels, level + 1):
        out = (f32(BW, BW),) + out
    if not early(levels, level):
        work += [vmem(BW, BW), vmem(8 * SLOTS, BW)]
    if len(theirs) == 2:
        work += [vmem(2 * part_rows(below), BW)]
    return pl.pallas_call(
        functools.partial(merge_kernel, levels, level),
        out_shape=out,
        in_specs=[SCALARS, SCALARS, WHOLE] + [WHOLE] * (len(theirs) + len(ahead)),
        out_specs=(WHOLE,) * len(out),
        scratch_shapes=work,
        compiler_params=PARAMS,
        name=f"merge_{level}",
    )(core, plan, own, *ahead, *theirs)


def recover(levels, plan, couplings, reduced, leaf):
    return pl.pallas_call(
        functools.partial(recover_kernel, levels),
        out_shape=f32(8, FW),
        in_specs=[SCALARS] + [WHOLE] * (2 * levels),
        out_specs=WHOLE,
        compiler_params=PARAMS,
        name="recover",
    )(plan, *couplings, *reduced, leaf)


def partner(block, axis, bit):
    count = lax.axis_size(axis)
    return lax.ppermute(block, axis, [(k, k ^ (1 << bit)) for k in range(count)])


def shards(leaf_matrix, leaf_source, observe, zone_ids, log_perm, block_map):
    leaf_count = lax.axis_size("leaf")
    devices = leaf_count * lax.axis_size("sub")
    leaf_bits = leaf_count.bit_length() - 1
    levels = devices.bit_length() - 1
    tree = (lax.axis_index("leaf") + leaf_count * lax.axis_index("sub")).astype(jnp.int32)[None]
    core = tree & 1
    plan = make_plan(levels, tree, block_map.reshape(-1))
    zones = jnp.broadcast_to(log_perm[None], (devices, log_perm.shape[0]))
    all_zones = lax.all_to_all(zones, ("leaf", "sub"), 0, 0, tiled=True).reshape(-1)
    cells = zone_ids[0]
    perm = jnp.exp(all_zones[cells])
    leaf, pack = leaf_front(levels, plan, leaf_matrix[0], leaf_source, observe, perm[None])
    front, couplings, reduced = leaf, [], []
    for level in range(levels):
        axis, bit = ("leaf", level) if level < leaf_bits else ("sub", level - leaf_bits)
        ahead = ()
        if early(levels, level):
            ahead = (shared_inverse(level, plan, lead, partner(lead, axis, bit)),)
        theirs = (partner(pack, axis, bit),)
        if level > 0 and parts(active(levels, level)) == 2:
            if ahead:
                theirs, ahead = lax.optimization_barrier((theirs, ahead))
            theirs += (partner(theirs[0], "leaf", 0),)
        more = list(merge(levels, level, core, plan, front, theirs, ahead))
        if early(levels, level + 1):
            lead = more.pop(0)
        if level < levels - 1:
            *more, front, pack = more
        couplings += more[:-1]
        reduced += more[-1:]
    solution = recover(levels, plan, couplings, reduced, leaf)
    terms = -perm * solution[0] * solution[1]
    partial = jax.ops.segment_sum(terms, cells, num_segments=all_zones.shape[0])
    shares = lax.all_to_all(partial.reshape(devices, -1), ("leaf", "sub"), 0, 0, tiled=True)
    return solution[0][None, :], shares.sum(0)


def solution(mesh):
    split_all = ("leaf", "sub")
    in_specs = (P(split_all, None, None), P(split_all, None), P(split_all, None), P(split_all, None), P(split_all), P())
    out_specs = (P(split_all, None), P(split_all))
    return jax.shard_map(shards, mesh=mesh, in_specs=in_specs, out_specs=out_specs, check_vma=False)
```

```python
import functools

import jax
import jax.numpy as jnp
from jax import lax
from jax.experimental import pallas as pl
from jax.experimental.pallas import tpu as pltpu
from jax.sharding import PartitionSpec as P

BW = 128
BW_BITS = 7
NB = 4
KEEP = NB - 1
FW = NB * BW
SLOTS = 64
NEVER = 99
STRIDE = 16
VMEM_LIMIT = 48 * 1024 * 1024


def split(x):
    high = x.astype(jnp.bfloat16)
    return high, (x - high.astype(jnp.float32)).astype(jnp.bfloat16)


def split_exact(x):
    high, low = split(x)
    rest = x - high.astype(jnp.float32)
    return high, low, (rest - low.astype(jnp.float32)).astype(jnp.bfloat16)


def one_hot(cells, width):
    row = lax.broadcasted_iota(jnp.int32, (width, cells.shape[1]), 0)
    return row == jnp.broadcast_to(cells, row.shape)


def dot_split(a, b):
    one = functools.partial(jnp.dot, preferred_element_type=jnp.float32)
    both = one(jnp.concatenate([a[0], a[1]], 1), jnp.concatenate([b[0], b[0]], 0))
    return both + one(a[0], b[1])


def dot_split_left(a, b):
    one = functools.partial(
        lax.dot_general, dimension_numbers=(((0,), (0,)), ((), ())), preferred_element_type=jnp.float32
    )
    both = one(jnp.concatenate([a[0], a[1]], 0), jnp.concatenate([b[0], b[0]], 0))
    return both + one(a[0], b[1])


def dot_split_right(a, b):
    one = functools.partial(
        lax.dot_general, dimension_numbers=(((1,), (1,)), ((), ())), preferred_element_type=jnp.float32
    )
    both = one(jnp.concatenate([a[0], a[1]], 1), jnp.concatenate([b[0], b[0]], 1))
    return both + one(a[0], b[1])


def lanes(x, c):
    return jnp.broadcast_to(x[:, c : c + 1], (8, BW))


def rows(x, j):
    return jnp.broadcast_to(x[j : j + 1, :], (8, BW))


def pivots(row, cols, sub, buffer, slot):
    def pair(v, j):
        slot[0] = (slot[0] + 1) % SLOTS
        at = 8 * slot[0]
        buffer[at : at + 8, :] = v
        return [jnp.broadcast_to(buffer[at + i : at + i + 1, :], (8, BW)) for i in (j, j + 1)]

    for j in range(0, 8, 2):
        left, right = cols[j], cols[j + 1]
        spread = {m: pair(cols[m], j) for m in range(j, 8)}
        a, b, c = spread[j][0], spread[j][1], spread[j + 1][1]
        scale = 1.0 / (a * c - b * b)
        first, second = sub == j, sub == j + 1

        def update(v, v0, v1):
            u0 = c * v0 - b * v1
            u1 = a * v1 - b * v0
            t = left * u0 + right * u1
            return jnp.where(first, u0 * scale, jnp.where(second, u1 * scale, v - t * scale))

        row = update(row, *pair(row, j))
        for m in range(j + 2, 8):
            cols[m] = update(cols[m], *spread[m])
    return row


def invert(slabs, buffer):
    lane = lax.broadcasted_iota(jnp.int32, (8, BW), 1)
    sub = lax.broadcasted_iota(jnp.int32, (8, BW), 0)
    slabs = list(slabs)
    count = len(slabs)
    half = count // 2
    slot = [0]
    for panel in (range(half), range(half, count)):
        for k in panel:
            cols = [lanes(slabs[k], 8 * k + j) for j in range(8)]
            inside = (lane >= 8 * k) & (lane < 8 * k + 8)
            row = jnp.where(lane == sub + 8 * k, 1.0, jnp.where(inside, 0.0, slabs[k]))
            row = pivots(row, cols, sub, buffer, slot)
            w = [rows(row, j) for j in range(8)]
            for r in [r for r in panel if r > k] + [r for r in panel if r < k]:
                t0 = jnp.where(inside, 0.0, slabs[r]) - lanes(slabs[r], 8 * k) * w[0]
                t1 = lanes(slabs[r], 8 * k + 1) * w[1]
                for j in range(2, 8, 2):
                    t0 = t0 - lanes(slabs[r], 8 * k + j) * w[j]
                    t1 = t1 + lanes(slabs[r], 8 * k + j + 1) * w[j + 1]
                slabs[r] = t0 - t1
            slabs[k] = row
        start, stop = 8 * panel[0], 8 * panel[-1] + 8
        inside = (lane >= start) & (lane < stop)
        rest = [r for r in range(count) if r not in panel]
        g = jnp.concatenate([slabs[r][:, start:stop] for r in rest], 0)
        change = dot_split(split(g), split(jnp.concatenate([slabs[r] for r in panel], 0)))
        for n, r in enumerate(rest):
            slabs[r] = jnp.where(inside, 0.0, slabs[r]) - change[8 * n : 8 * n + 8]
    return slabs


def span(block):
    return pl.ds(pl.multiple_of(block * BW, BW), BW)


def invert_ref(load, store, buffer):
    out = invert([load(8 * r) for r in range(BW // 8)], buffer)
    for r in range(BW // 8):
        store[8 * r : 8 * r + 8, :] = out[r]


def sweep(front, inverse, wide, buffer, block):
    at = pl.multiple_of(block * BW, BW)
    invert_ref(lambda r: front[pl.ds(at + r, 8), pl.ds(at, BW)], inverse, buffer)
    wide[...] = dot_split(split(inverse[...]), split(front[pl.ds(at, BW), :]))
    wide[:, pl.ds(at, BW)] = inverse[...]
    w = split(wide[...])
    for start, size in [(i * BW, BW) for i in range(NB)] + [(FW, 8)]:
        g = split(front[start : start + size, pl.ds(at, BW)])
        front[start : start + size, pl.ds(at, BW)] = jnp.zeros((size, BW), jnp.float32)
        front[start : start + size, :] -= dot_split(g, w)


def active(levels, level):
    return min(NB, levels - level)


def pairs(count):
    return [(a, b) for a in range(count) for b in range(a, count)]


def parts(count):
    return 1 if count * (count + 1) // 2 % 2 else 2


def part_rows(count):
    return len(pairs(count)) // parts(count) * BW + -(-count // parts(count)) * 8


def block_row(count, p):
    each = len(pairs(count)) // parts(count)
    return p // each * part_rows(count) + p % each * BW


def rhs_row(count, a):
    each = -(-count // parts(count))
    return a // each * part_rows(count) + len(pairs(count)) // parts(count) * BW + a % each * 8


def write_pack(front, pack, count, core, at, rhs, valid):
    size = part_rows(count)
    whole = pack.shape[0] == parts(count) * size

    def put(start, height, source, ok):
        part = start // size
        to = start if whole else start % size
        ok = ok if whole else ok & (core == part)

        @pl.when(ok)
        def _():
            pack[to : to + height, :] = source()

    for p, (a, b) in enumerate(pairs(count)):
        put(block_row(count, p), BW, lambda a=a, b=b: front[at(a), at(b)], valid(a) & valid(b))
    for a in range(count):
        put(rhs_row(count, a), 8, lambda a=a: front[rhs : rhs + 8, at(a)], valid(a))


def plan_kernel(levels, tree_ref, map_ref, plan, when, position):
    tree = tree_ref[0]
    for i in range(NB):
        when[levels * NB + i] = NEVER
        position[levels * NB + i] = -1
    for level in reversed(range(levels)):
        nodes, node = (1 << levels) >> level, tree >> level
        mine, yours = (
            [map_ref[(nodes + n - 2) * NB + i] for i in range(NB)] for n in (node, node ^ 1)
        )
        dropped = active(levels, level + 1)
        for child, other, base in ((mine, yours, 0), (yours, mine, 4)):
            after, spot, place = [], [], []
            for m in child:
                both = functools.reduce(jnp.logical_or, [m == o for o in other])
                above = (level + 1) * NB + jnp.maximum(m - KEEP, 0)
                later = jnp.where(m >= KEEP, when[above], NEVER)
                after.append(jnp.where(both, level, later))
                place.append(jnp.where(later < NEVER, position[above], jnp.where(both, dropped, -1)))
            for i in range(NB):
                ahead = functools.reduce(jnp.add, [jnp.where(after[k] < after[i], 1, 0) for k in range(NB) if k != i])
                spot.append(jnp.where(after[i] < NEVER, ahead, -1))
            for a in range(NB):
                slot, order = jnp.int32(-1), jnp.int32(-1)
                for i in range(NB):
                    slot = jnp.where(spot[i] == a, place[i], slot)
                    order = jnp.where(spot[i] == a, i, order)
                plan[level * STRIDE + base + a] = slot
                if level == 0 and base == 0:
                    plan[levels * STRIDE + a] = order
            if base == 0:
                for i in range(NB):
                    when[level * NB + i] = after[i]
                    position[level * NB + i] = spot[i]
                    if level == 0:
                        plan[levels * STRIDE + 4 + i] = spot[i]
        plan[level * STRIDE + 8] = jnp.where(plan[level * STRIDE] == dropped, 1, 0)


def leaf_kernel(levels, plan, leaf, source, observe, zones, cells, front, pack, perm, inverse, wide, buffer):
    owner = one_hot(cells[...] >> BW_BITS, zones.shape[0]).astype(jnp.float32).astype(jnp.bfloat16)
    held = sum(
        lax.dot_general(part, owner, (((0,), (0,)), ((), ())), preferred_element_type=jnp.float32)
        for part in split_exact(zones[...])
    )
    within = one_hot(cells[...] & (BW - 1), BW)
    perm[...] = jnp.exp(jnp.sum(jnp.where(within, held, 0.0), axis=0, keepdims=True))
    front[0:FW, :] = leaf[...]
    eye = lax.broadcasted_iota(jnp.int32, (BW, BW), 0) == lax.broadcasted_iota(jnp.int32, (BW, BW), 1)
    for i in range(NB):
        at = slice(i * BW, i * BW + BW)
        front[at, at] += jnp.where(eye, jnp.broadcast_to(perm[:, at], (BW, BW)), 0.0)
    which = lax.broadcasted_iota(jnp.int32, (8, FW), 0)
    front[FW : FW + 8, :] = jnp.where(
        which == 0,
        jnp.broadcast_to(source[...], (8, FW)),
        jnp.where(which == 1, jnp.broadcast_to(observe[...], (8, FW)), 0.0),
    )
    order = [plan[levels * STRIDE + a] for a in range(NB)]

    def step(i, carry):
        @pl.when(plan[levels * STRIDE + 4 + i] < 0)
        def _():
            sweep(front, inverse, wide, buffer, i)

        return carry

    lax.fori_loop(0, NB, step, 0)
    count = active(levels, 0)
    write_pack(
        front, pack, count, 0, lambda a: span(jnp.maximum(order[a], 0)), FW, lambda a: order[a] >= 0
    )


def inverse_kernel(level, plan, own, theirs, inverse, buffer):
    @pl.when(plan[level * STRIDE + 8] == 1)
    def _():
        inverse[...] = own[...] + theirs[...]
        invert_ref(lambda r: inverse[r : r + 8, :], inverse, buffer)


def early(levels, level):
    return False


def merge_kernel(levels, level, core_ref, plan, own, *rest):
    if early(levels, level):
        ahead, *rest = rest
    below, count = active(levels, level), active(levels, level + 1)
    core = core_ref[0]
    base = level * STRIDE
    if level > 0 and parts(below) == 2:
        same, swapped, *rest, theirs = rest
        size = part_rows(below)
        theirs[pl.ds(pl.multiple_of(core * size, 8), size), :] = same[...]
        theirs[pl.ds(pl.multiple_of((1 - core) * size, 8), size), :] = swapped[...]
    else:
        theirs, *rest = rest
    if not early(levels, level):
        *rest, ahead, buffer = rest
    if early(levels, level + 1):
        lead, *rest = rest
    if count:
        coupling, reduced, front, pack, diagonal, coupled = rest
        front[...] = jnp.zeros(front.shape, jnp.float32)
        coupled[...] = jnp.zeros(coupled.shape, jnp.float32)
    else:
        reduced, diagonal = rest
    mine = [plan[base + a] for a in range(below)]
    yours = [plan[base + 4 + a] for a in range(below)]
    eliminated = plan[base + 8] == 1
    kept = plan[base + 8] == 0
    rhs = count * BW
    if level == 0:
        order = [jnp.maximum(plan[levels * STRIDE + a], 0) for a in range(below)]
        at, own_rhs = lambda a: span(order[a]), FW
    else:
        at, own_rhs = lambda a: slice(a * BW, a * BW + BW), below * BW
    their_rows = {p: block_row(below, n) for n, p in enumerate(pairs(below))}
    their_block = lambda a, b: theirs[their_rows[a, b] : their_rows[a, b] + BW, :]
    their_rhs = lambda a: theirs[rhs_row(below, a) : rhs_row(below, a) + 8, :]
    diagonal[...] = own[at(0), at(0)] + their_block(0, 0)
    right = own[own_rhs : own_rhs + 8, at(0)] + their_rhs(0)
    reduced[...] = right

    def put(ok, a, b, value):
        @pl.when(ok)
        def _():
            front[span(a), span(b)] = value()

    def put_rhs(ok, a, value):
        @pl.when(ok)
        def _():
            front[rhs : rhs + 8, span(a)] = value()

    if count:
        put(kept, mine[0], mine[0], lambda: diagonal[...])
        put_rhs(kept, mine[0], lambda: reduced[...])
        for a in range(1, below):
            for slots, block, across, vector in (
                (mine, lambda a, b: own[at(a), at(b)], lambda a, b: own[at(b), at(a)], lambda a: own[own_rhs : own_rhs + 8, at(a)]),
                (yours, their_block, lambda a, b: their_block(a, b).T, their_rhs),
            ):
                there = slots[a] >= 0

                @pl.when(there & eliminated)
                def _():
                    coupled[:, span(slots[a])] = block(0, a)

                put(there & kept, slots[0], slots[a], lambda: block(0, a))
                put(there & kept, slots[a], slots[0], lambda: across(0, a))
                put_rhs(there, slots[a], lambda: vector(a))
                for b in range(a, below):
                    both = there & (slots[b] >= 0)
                    put(both, slots[a], slots[b], lambda: block(a, b))
                    if a != b:
                        put(both, slots[b], slots[a], lambda: across(a, b))

    @pl.when(eliminated)
    def _():
        if not early(levels, level):
            invert_ref(lambda r: diagonal[r : r + 8, :], ahead, buffer)
        d, r = split(ahead[...]), split(reduced[...])
        if count:
            c = split(coupled[...])
            w = dot_split(d, c)
            coupling[...] = w
            w = split(w)
            front[0:rhs, :] -= dot_split_left(c, w)
            front[rhs : rhs + 8, :] -= dot_split(r, w)
        reduced[...] = dot_split(r, d)

    if count:

        @pl.when(kept)
        def _():
            coupling[...] = jnp.zeros(coupling.shape, jnp.float32)

        write_pack(
            front, pack, count, core, lambda a: slice(a * BW, a * BW + BW), rhs, lambda a: plan[0] == plan[0]
        )
        if early(levels, level + 1):
            lead[...] = front[0:BW, 0:BW]


def pick(blocks, slot):
    out = jnp.zeros((8, BW), jnp.float32)
    for n, block in enumerate(blocks):
        out = jnp.where(slot == n, block, out)
    return out


def recover_kernel(levels, plan, *refs):
    couplings, reduced = refs[: levels - 1], refs[levels - 1 : 2 * levels - 1]
    leaf, perm, cells, out, partial = refs[2 * levels - 1 :]
    solved = [reduced[levels - 1][...]]
    for level in reversed(range(1, levels)):
        kept = [pick(solved, plan[level * STRIDE + a]) for a in range(active(levels, level))]
        z = split(jnp.concatenate(kept, 1))
        solved = kept + [reduced[level - 1][...] - dot_split_right(z, split(couplings[level - 1][...]))]
    spots = [plan[levels * STRIDE + 4 + i] for i in range(NB)]
    kept = [pick(solved, jnp.where(spot >= 0, plan[jnp.maximum(spot, 0)], -1)) for spot in spots]
    new = dot_split(split(jnp.concatenate(kept, 1)), split(leaf[0:FW, :])) - leaf[FW : FW + 8, :]
    both = jnp.concatenate(
        [jnp.where(spots[i] >= 0, kept[i], new[:, i * BW : i * BW + BW]) for i in range(NB)], 1
    )
    out[...] = both[0:1]
    terms = -perm[...] * both[0:1] * both[1:2]
    owner = one_hot(cells[...] >> BW_BITS, partial.shape[0]).astype(jnp.float32).astype(jnp.bfloat16)
    within = one_hot(cells[...] & (BW - 1), BW)
    spread = jnp.where(within, jnp.broadcast_to(terms, within.shape), 0.0)
    partial[...] = sum(
        lax.dot_general(owner, part, (((1,), (1,)), ((), ())), preferred_element_type=jnp.float32)
        for part in split_exact(spread)
    )


SCALARS = pl.BlockSpec(memory_space=pltpu.SMEM)
WHOLE = pl.BlockSpec(memory_space=pltpu.VMEM)
PARAMS = pltpu.CompilerParams(vmem_limit_bytes=VMEM_LIMIT)


def f32(*shape):
    return jax.ShapeDtypeStruct(shape, jnp.float32)


def vmem(*shape):
    return pltpu.VMEM(shape, jnp.float32)


def make_plan(levels, tree, maps):
    return pl.pallas_call(
        functools.partial(plan_kernel, levels),
        out_shape=jax.ShapeDtypeStruct(((levels + 1) * STRIDE,), jnp.int32),
        in_specs=[SCALARS, SCALARS],
        out_specs=SCALARS,
        scratch_shapes=[pltpu.SMEM(((levels + 1) * NB,), jnp.int32)] * 2,
        name="make_plan",
    )(tree, maps)


def leaf_front(levels, plan, leaf, source, observe, zones, cells):
    count = active(levels, 0)
    return pl.pallas_call(
        functools.partial(leaf_kernel, levels),
        out_shape=(f32(FW + 8, FW), f32(parts(count) * part_rows(count), BW), f32(1, FW)),
        in_specs=[SCALARS] + [WHOLE] * 5,
        out_specs=(WHOLE,) * 3,
        scratch_shapes=[vmem(BW, BW), vmem(BW, FW), vmem(8 * SLOTS, BW)],
        compiler_params=PARAMS,
        name="leaf_front",
    )(plan, leaf, source, observe, zones, cells)


def shared_inverse(level, plan, own, theirs):
    return pl.pallas_call(
        functools.partial(inverse_kernel, level),
        out_shape=f32(BW, BW),
        in_specs=[SCALARS, WHOLE, WHOLE],
        out_specs=WHOLE,
        scratch_shapes=[vmem(8 * SLOTS, BW)],
        compiler_params=PARAMS,
        cost_estimate=pl.CostEstimate(flops=4 * BW**3, bytes_accessed=12 * BW * BW, transcendentals=0),
        name=f"inverse_{level}",
    )(plan, own, theirs)


def merge(levels, level, core, plan, own, theirs, ahead):
    below, count = active(levels, level), active(levels, level + 1)
    n = count * BW
    out, work = (f32(8, BW),), [vmem(BW, BW)]
    if count:
        out = (f32(BW, n),) + out + (f32(n + 8, n), f32(part_rows(count), BW))
        work += [vmem(BW, n)]
    if early(levels, level + 1):
        out = (f32(BW, BW),) + out
    if not early(levels, level):
        work += [vmem(BW, BW), vmem(8 * SLOTS, BW)]
    if len(theirs) == 2:
        work += [vmem(2 * part_rows(below), BW)]
    return pl.pallas_call(
        functools.partial(merge_kernel, levels, level),
        out_shape=out,
        in_specs=[SCALARS, SCALARS, WHOLE] + [WHOLE] * (len(theirs) + len(ahead)),
        out_specs=(WHOLE,) * len(out),
        scratch_shapes=work,
        compiler_params=PARAMS,
        name=f"merge_{level}",
    )(core, plan, own, *ahead, *theirs)


def recover(levels, plan, couplings, reduced, leaf, perm, cells):
    return pl.pallas_call(
        functools.partial(recover_kernel, levels),
        out_shape=(f32(1, FW), f32(1 << levels, BW)),
        in_specs=[SCALARS] + [WHOLE] * (2 * levels + 2),
        out_specs=(WHOLE, WHOLE),
        compiler_params=PARAMS,
        name="recover",
    )(plan, *couplings, *reduced, leaf, perm, cells)


def partner(block, axis, bit):
    count = lax.axis_size(axis)
    return lax.ppermute(block, axis, [(k, k ^ (1 << bit)) for k in range(count)])


def shards(leaf_matrix, leaf_source, observe, zone_ids, log_perm, block_map):
    leaf_count = lax.axis_size("leaf")
    devices = leaf_count * lax.axis_size("sub")
    leaf_bits = leaf_count.bit_length() - 1
    levels = devices.bit_length() - 1
    tree = (lax.axis_index("leaf") + leaf_count * lax.axis_index("sub")).astype(jnp.int32)[None]
    core = tree & 1
    plan = make_plan(levels, tree, block_map.reshape(-1))
    zones = jnp.broadcast_to(log_perm[None], (devices, log_perm.shape[0]))
    all_zones = lax.all_to_all(zones, ("leaf", "sub"), 0, 0, tiled=True)
    leaf, pack, perm = leaf_front(levels, plan, leaf_matrix[0], leaf_source, observe, all_zones, zone_ids)
    front, couplings, reduced = leaf, [], []
    for level in range(levels):
        axis, bit = ("leaf", level) if level < leaf_bits else ("sub", level - leaf_bits)
        ahead = ()
        if early(levels, level):
            ahead = (shared_inverse(level, plan, lead, partner(lead, axis, bit)),)
        theirs = (partner(pack, axis, bit),)
        if level > 0 and parts(active(levels, level)) == 2:
            if ahead:
                theirs, ahead = lax.optimization_barrier((theirs, ahead))
            theirs += (partner(theirs[0], "leaf", 0),)
        more = list(merge(levels, level, core, plan, front, theirs, ahead))
        if early(levels, level + 1):
            lead = more.pop(0)
        if level < levels - 1:
            *more, front, pack = more
        couplings += more[:-1]
        reduced += more[-1:]
    solution, partial = recover(levels, plan, couplings, reduced, leaf, perm, zone_ids)
    shares = lax.all_to_all(partial, ("leaf", "sub"), 0, 0, tiled=True)
    return solution, shares.sum(0)


def solution(mesh):
    split_all = ("leaf", "sub")
    in_specs = (P(split_all, None, None), P(split_all, None), P(split_all, None), P(split_all, None), P(split_all), P())
    out_specs = (P(split_all, None), P(split_all))
    return jax.shard_map(shards, mesh=mesh, in_specs=in_specs, out_specs=out_specs, check_vma=False)
```

```python
import functools

import jax
import jax.numpy as jnp
from jax import lax
from jax.experimental import pallas as pl
from jax.experimental.pallas import tpu as pltpu
from jax.sharding import PartitionSpec as P

BW = 128
BW_BITS = 7
NB = 4
KEEP = NB - 1
FW = NB * BW
SLOTS = 64
NEVER = 99
STRIDE = 16
VMEM_LIMIT = 48 * 1024 * 1024


def split(x):
    high = x.astype(jnp.bfloat16)
    return high, (x - high.astype(jnp.float32)).astype(jnp.bfloat16)


def split_exact(x):
    high, low = split(x)
    rest = x - high.astype(jnp.float32)
    return high, low, (rest - low.astype(jnp.float32)).astype(jnp.bfloat16)


def one_hot(cells, width):
    row = lax.broadcasted_iota(jnp.int32, (width, cells.shape[1]), 0)
    return row == jnp.broadcast_to(cells, row.shape)


def dot_split(a, b):
    one = functools.partial(jnp.dot, preferred_element_type=jnp.float32)
    both = one(jnp.concatenate([a[0], a[1]], 1), jnp.concatenate([b[0], b[0]], 0))
    return both + one(a[0], b[1])


def dot_split_left(a, b):
    one = functools.partial(
        lax.dot_general, dimension_numbers=(((0,), (0,)), ((), ())), preferred_element_type=jnp.float32
    )
    both = one(jnp.concatenate([a[0], a[1]], 0), jnp.concatenate([b[0], b[0]], 0))
    return both + one(a[0], b[1])


def dot_split_right(a, b):
    one = functools.partial(
        lax.dot_general, dimension_numbers=(((1,), (1,)), ((), ())), preferred_element_type=jnp.float32
    )
    both = one(jnp.concatenate([a[0], a[1]], 1), jnp.concatenate([b[0], b[0]], 1))
    return both + one(a[0], b[1])


def lanes(x, c):
    return jnp.broadcast_to(x[:, c : c + 1], (8, BW))


def rows(x, j):
    return jnp.broadcast_to(x[j : j + 1, :], (8, BW))


def pivots(row, cols, sub, buffer, slot):
    def pair(v, j):
        slot[0] = (slot[0] + 1) % SLOTS
        at = 8 * slot[0]
        buffer[at : at + 8, :] = v
        return [jnp.broadcast_to(buffer[at + i : at + i + 1, :], (8, BW)) for i in (j, j + 1)]

    for j in range(0, 8, 2):
        left, right = cols[j], cols[j + 1]
        spread = {m: pair(cols[m], j) for m in range(j, 8)}
        a, b, c = spread[j][0], spread[j][1], spread[j + 1][1]
        scale = 1.0 / (a * c - b * b)
        first, second = sub == j, sub == j + 1

        def update(v, v0, v1):
            u0 = c * v0 - b * v1
            u1 = a * v1 - b * v0
            t = left * u0 + right * u1
            return jnp.where(first, u0 * scale, jnp.where(second, u1 * scale, v - t * scale))

        row = update(row, *pair(row, j))
        for m in range(j + 2, 8):
            cols[m] = update(cols[m], *spread[m])
    return row


def invert(slabs, buffer):
    lane = lax.broadcasted_iota(jnp.int32, (8, BW), 1)
    sub = lax.broadcasted_iota(jnp.int32, (8, BW), 0)
    slabs = list(slabs)
    count = len(slabs)
    half = count // 2
    slot = [0]
    for panel in (range(half), range(half, count)):
        for k in panel:
            cols = [lanes(slabs[k], 8 * k + j) for j in range(8)]
            inside = (lane >= 8 * k) & (lane < 8 * k + 8)
            row = jnp.where(lane == sub + 8 * k, 1.0, jnp.where(inside, 0.0, slabs[k]))
            row = pivots(row, cols, sub, buffer, slot)
            w = [rows(row, j) for j in range(8)]
            for r in [r for r in panel if r > k] + [r for r in panel if r < k]:
                t0 = jnp.where(inside, 0.0, slabs[r]) - lanes(slabs[r], 8 * k) * w[0]
                t1 = lanes(slabs[r], 8 * k + 1) * w[1]
                for j in range(2, 8, 2):
                    t0 = t0 - lanes(slabs[r], 8 * k + j) * w[j]
                    t1 = t1 + lanes(slabs[r], 8 * k + j + 1) * w[j + 1]
                slabs[r] = t0 - t1
            slabs[k] = row
        start, stop = 8 * panel[0], 8 * panel[-1] + 8
        inside = (lane >= start) & (lane < stop)
        rest = [r for r in range(count) if r not in panel]
        g = jnp.concatenate([slabs[r][:, start:stop] for r in rest], 0)
        change = dot_split(split(g), split(jnp.concatenate([slabs[r] for r in panel], 0)))
        for n, r in enumerate(rest):
            slabs[r] = jnp.where(inside, 0.0, slabs[r]) - change[8 * n : 8 * n + 8]
    return slabs


def span(block):
    return pl.ds(pl.multiple_of(block * BW, BW), BW)


def invert_ref(load, store, buffer):
    out = invert([load(8 * r) for r in range(BW // 8)], buffer)
    for r in range(BW // 8):
        store[8 * r : 8 * r + 8, :] = out[r]


def sweep(front, inverse, wide, buffer, block):
    at = pl.multiple_of(block * BW, BW)
    invert_ref(lambda r: front[pl.ds(at + r, 8), pl.ds(at, BW)], inverse, buffer)
    wide[...] = dot_split(split(inverse[...]), split(front[pl.ds(at, BW), :]))
    wide[:, pl.ds(at, BW)] = inverse[...]
    w = split(wide[...])
    for start, size in [(i * BW, BW) for i in range(NB)] + [(FW, 8)]:
        g = split(front[start : start + size, pl.ds(at, BW)])
        front[start : start + size, pl.ds(at, BW)] = jnp.zeros((size, BW), jnp.float32)
        front[start : start + size, :] -= dot_split(g, w)


def active(levels, level):
    return min(NB, levels - level)


def pairs(count):
    return [(a, b) for a in range(count) for b in range(a, count)]


def parts(count):
    return 1 if count * (count + 1) // 2 % 2 else 2


def part_rows(count):
    return len(pairs(count)) // parts(count) * BW + -(-count // parts(count)) * 8


def block_row(count, p):
    each = len(pairs(count)) // parts(count)
    return p // each * part_rows(count) + p % each * BW


def rhs_row(count, a):
    each = -(-count // parts(count))
    return a // each * part_rows(count) + len(pairs(count)) // parts(count) * BW + a % each * 8


def write_pack(front, pack, count, core, at, rhs, valid):
    size = part_rows(count)
    whole = pack.shape[0] == parts(count) * size

    def put(start, height, source, ok):
        part = start // size
        to = start if whole else start % size
        ok = ok if whole else ok & (core == part)

        @pl.when(ok)
        def _():
            pack[to : to + height, :] = source()

    for p, (a, b) in enumerate(pairs(count)):
        put(block_row(count, p), BW, lambda a=a, b=b: front[at(a), at(b)], valid(a) & valid(b))
    for a in range(count):
        put(rhs_row(count, a), 8, lambda a=a: front[rhs : rhs + 8, at(a)], valid(a))


def plan_kernel(levels, tree_ref, map_ref, plan, when, position):
    tree = tree_ref[0]
    for i in range(NB):
        when[levels * NB + i] = NEVER
        position[levels * NB + i] = -1
    for level in reversed(range(levels)):
        nodes, node = (1 << levels) >> level, tree >> level
        mine, yours = (
            [map_ref[nodes + n - 2, i] for i in range(NB)] for n in (node, node ^ 1)
        )
        dropped = active(levels, level + 1)
        for child, other, base in ((mine, yours, 0), (yours, mine, 4)):
            after, spot, place = [], [], []
            for m in child:
                both = functools.reduce(jnp.logical_or, [m == o for o in other])
                above = (level + 1) * NB + jnp.maximum(m - KEEP, 0)
                later = jnp.where(m >= KEEP, when[above], NEVER)
                after.append(jnp.where(both, level, later))
                place.append(jnp.where(later < NEVER, position[above], jnp.where(both, dropped, -1)))
            for i in range(NB):
                ahead = functools.reduce(jnp.add, [jnp.where(after[k] < after[i], 1, 0) for k in range(NB) if k != i])
                spot.append(jnp.where(after[i] < NEVER, ahead, -1))
            for a in range(NB):
                slot, order = jnp.int32(-1), jnp.int32(-1)
                for i in range(NB):
                    slot = jnp.where(spot[i] == a, place[i], slot)
                    order = jnp.where(spot[i] == a, i, order)
                plan[level * STRIDE + base + a] = slot
                if level == 0 and base == 0:
                    plan[levels * STRIDE + a] = order
            if base == 0:
                for i in range(NB):
                    when[level * NB + i] = after[i]
                    position[level * NB + i] = spot[i]
                    if level == 0:
                        plan[levels * STRIDE + 4 + i] = spot[i]
        plan[level * STRIDE + 8] = jnp.where(plan[level * STRIDE] == dropped, 1, 0)


def leaf_kernel(levels, plan, leaf, source, observe, zones, cells, front, pack, perm, inverse, wide, buffer):
    owner = one_hot(cells[...] >> BW_BITS, zones.shape[0]).astype(jnp.float32).astype(jnp.bfloat16)
    held = sum(
        lax.dot_general(part, owner, (((0,), (0,)), ((), ())), preferred_element_type=jnp.float32)
        for part in split_exact(zones[...])
    )
    within = one_hot(cells[...] & (BW - 1), BW)
    perm[...] = jnp.exp(jnp.sum(jnp.where(within, held, 0.0), axis=0, keepdims=True))
    front[0:FW, :] = leaf[...]
    eye = lax.broadcasted_iota(jnp.int32, (BW, BW), 0) == lax.broadcasted_iota(jnp.int32, (BW, BW), 1)
    for i in range(NB):
        at = slice(i * BW, i * BW + BW)
        front[at, at] += jnp.where(eye, jnp.broadcast_to(perm[:, at], (BW, BW)), 0.0)
    which = lax.broadcasted_iota(jnp.int32, (8, FW), 0)
    front[FW : FW + 8, :] = jnp.where(
        which == 0,
        jnp.broadcast_to(source[...], (8, FW)),
        jnp.where(which == 1, jnp.broadcast_to(observe[...], (8, FW)), 0.0),
    )
    order = [plan[levels * STRIDE + a] for a in range(NB)]

    def step(i, carry):
        @pl.when(plan[levels * STRIDE + 4 + i] < 0)
        def _():
            sweep(front, inverse, wide, buffer, i)

        return carry

    lax.fori_loop(0, NB, step, 0)
    count = active(levels, 0)
    write_pack(
        front, pack, count, 0, lambda a: span(jnp.maximum(order[a], 0)), FW, lambda a: order[a] >= 0
    )


def inverse_kernel(level, plan, own, theirs, inverse, buffer):
    @pl.when(plan[level * STRIDE + 8] == 1)
    def _():
        inverse[...] = own[...] + theirs[...]
        invert_ref(lambda r: inverse[r : r + 8, :], inverse, buffer)


def early(levels, level):
    return False


def merge_kernel(levels, level, core_ref, plan, own, *rest):
    if early(levels, level):
        ahead, *rest = rest
    below, count = active(levels, level), active(levels, level + 1)
    core = core_ref[0]
    base = level * STRIDE
    if level > 0 and parts(below) == 2:
        same, swapped, *rest, theirs = rest
        size = part_rows(below)
        theirs[pl.ds(pl.multiple_of(core * size, 8), size), :] = same[...]
        theirs[pl.ds(pl.multiple_of((1 - core) * size, 8), size), :] = swapped[...]
    else:
        theirs, *rest = rest
    if not early(levels, level):
        *rest, ahead, buffer = rest
    if early(levels, level + 1):
        lead, *rest = rest
    if count:
        coupling, reduced, front, pack, diagonal, coupled = rest
        front[...] = jnp.zeros(front.shape, jnp.float32)
        coupled[...] = jnp.zeros(coupled.shape, jnp.float32)
    else:
        reduced, diagonal = rest
    mine = [plan[base + a] for a in range(below)]
    yours = [plan[base + 4 + a] for a in range(below)]
    eliminated = plan[base + 8] == 1
    kept = plan[base + 8] == 0
    rhs = count * BW
    if level == 0:
        order = [jnp.maximum(plan[levels * STRIDE + a], 0) for a in range(below)]
        at, own_rhs = lambda a: span(order[a]), FW
    else:
        at, own_rhs = lambda a: slice(a * BW, a * BW + BW), below * BW
    their_rows = {p: block_row(below, n) for n, p in enumerate(pairs(below))}
    their_block = lambda a, b: theirs[their_rows[a, b] : their_rows[a, b] + BW, :]
    their_rhs = lambda a: theirs[rhs_row(below, a) : rhs_row(below, a) + 8, :]
    diagonal[...] = own[at(0), at(0)] + their_block(0, 0)
    right = own[own_rhs : own_rhs + 8, at(0)] + their_rhs(0)
    reduced[...] = right

    def put(ok, a, b, value):
        @pl.when(ok)
        def _():
            front[span(a), span(b)] = value()

    def put_rhs(ok, a, value):
        @pl.when(ok)
        def _():
            front[rhs : rhs + 8, span(a)] = value()

    if count:
        put(kept, mine[0], mine[0], lambda: diagonal[...])
        put_rhs(kept, mine[0], lambda: reduced[...])
        for a in range(1, below):
            for slots, block, across, vector in (
                (mine, lambda a, b: own[at(a), at(b)], lambda a, b: own[at(b), at(a)], lambda a: own[own_rhs : own_rhs + 8, at(a)]),
                (yours, their_block, lambda a, b: their_block(a, b).T, their_rhs),
            ):
                there = slots[a] >= 0

                @pl.when(there & eliminated)
                def _():
                    coupled[:, span(slots[a])] = block(0, a)

                put(there & kept, slots[0], slots[a], lambda: block(0, a))
                put(there & kept, slots[a], slots[0], lambda: across(0, a))
                put_rhs(there, slots[a], lambda: vector(a))
                for b in range(a, below):
                    both = there & (slots[b] >= 0)
                    put(both, slots[a], slots[b], lambda: block(a, b))
                    if a != b:
                        put(both, slots[b], slots[a], lambda: across(a, b))

    @pl.when(eliminated)
    def _():
        if not early(levels, level):
            invert_ref(lambda r: diagonal[r : r + 8, :], ahead, buffer)
        d, r = split(ahead[...]), split(reduced[...])
        if count:
            c = split(coupled[...])
            w = dot_split(d, c)
            coupling[...] = w
            w = split(w)
            front[0:rhs, :] -= dot_split_left(c, w)
            front[rhs : rhs + 8, :] -= dot_split(r, w)
        reduced[...] = dot_split(r, d)

    if count:

        @pl.when(kept)
        def _():
            coupling[...] = jnp.zeros(coupling.shape, jnp.float32)

        write_pack(
            front, pack, count, core, lambda a: slice(a * BW, a * BW + BW), rhs, lambda a: plan[0] == plan[0]
        )
        if early(levels, level + 1):
            lead[...] = front[0:BW, 0:BW]


def pick(blocks, slot):
    out = jnp.zeros((8, BW), jnp.float32)
    for n, block in enumerate(blocks):
        out = jnp.where(slot == n, block, out)
    return out


def recover_kernel(levels, plan, *refs):
    couplings, reduced = refs[: levels - 1], refs[levels - 1 : 2 * levels - 1]
    leaf, perm, cells, out, partial = refs[2 * levels - 1 :]
    solved = [reduced[levels - 1][...]]
    for level in reversed(range(1, levels)):
        kept = [pick(solved, plan[level * STRIDE + a]) for a in range(active(levels, level))]
        z = split(jnp.concatenate(kept, 1))
        solved = kept + [reduced[level - 1][...] - dot_split_right(z, split(couplings[level - 1][...]))]
    spots = [plan[levels * STRIDE + 4 + i] for i in range(NB)]
    kept = [pick(solved, jnp.where(spot >= 0, plan[jnp.maximum(spot, 0)], -1)) for spot in spots]
    new = dot_split(split(jnp.concatenate(kept, 1)), split(leaf[0:FW, :])) - leaf[FW : FW + 8, :]
    both = jnp.concatenate(
        [jnp.where(spots[i] >= 0, kept[i], new[:, i * BW : i * BW + BW]) for i in range(NB)], 1
    )
    out[...] = both[0:1]
    terms = -perm[...] * both[0:1] * both[1:2]
    owner = one_hot(cells[...] >> BW_BITS, partial.shape[0]).astype(jnp.float32).astype(jnp.bfloat16)
    within = one_hot(cells[...] & (BW - 1), BW)
    spread = jnp.where(within, jnp.broadcast_to(terms, within.shape), 0.0)
    partial[...] = sum(
        lax.dot_general(owner, part, (((1,), (1,)), ((), ())), preferred_element_type=jnp.float32)
        for part in split_exact(spread)
    )


SCALARS = pl.BlockSpec(memory_space=pltpu.SMEM)
WHOLE = pl.BlockSpec(memory_space=pltpu.VMEM)
PARAMS = pltpu.CompilerParams(vmem_limit_bytes=VMEM_LIMIT)
LEAF_PARAMS = pltpu.CompilerParams(vmem_limit_bytes=62 * 1024 * 1024)


def f32(*shape):
    return jax.ShapeDtypeStruct(shape, jnp.float32)


def vmem(*shape):
    return pltpu.VMEM(shape, jnp.float32)


def make_plan(levels, tree, maps):
    return pl.pallas_call(
        functools.partial(plan_kernel, levels),
        out_shape=jax.ShapeDtypeStruct(((levels + 1) * STRIDE,), jnp.int32),
        in_specs=[SCALARS, SCALARS],
        out_specs=SCALARS,
        scratch_shapes=[pltpu.SMEM(((levels + 1) * NB,), jnp.int32)] * 2,
        name="make_plan",
    )(tree, maps)


def leaf_front(levels, plan, leaf, source, observe, zones, cells):
    count = active(levels, 0)
    return pl.pallas_call(
        functools.partial(leaf_kernel, levels),
        out_shape=(f32(FW + 8, FW), f32(parts(count) * part_rows(count), BW), f32(1, FW)),
        in_specs=[SCALARS] + [WHOLE] * 5,
        out_specs=(WHOLE,) * 3,
        scratch_shapes=[vmem(BW, BW), vmem(BW, FW), vmem(8 * SLOTS, BW)],
        compiler_params=LEAF_PARAMS,
        name="leaf_front",
    )(plan, leaf, source, observe, zones, cells)


def shared_inverse(level, plan, own, theirs):
    return pl.pallas_call(
        functools.partial(inverse_kernel, level),
        out_shape=f32(BW, BW),
        in_specs=[SCALARS, WHOLE, WHOLE],
        out_specs=WHOLE,
        scratch_shapes=[vmem(8 * SLOTS, BW)],
        compiler_params=PARAMS,
        cost_estimate=pl.CostEstimate(flops=4 * BW**3, bytes_accessed=12 * BW * BW, transcendentals=0),
        name=f"inverse_{level}",
    )(plan, own, theirs)


def merge(levels, level, core, plan, own, theirs, ahead):
    below, count = active(levels, level), active(levels, level + 1)
    n = count * BW
    out, work = (f32(8, BW),), [vmem(BW, BW)]
    if count:
        out = (f32(BW, n),) + out + (f32(n + 8, n), f32(part_rows(count), BW))
        work += [vmem(BW, n)]
    if early(levels, level + 1):
        out = (f32(BW, BW),) + out
    if not early(levels, level):
        work += [vmem(BW, BW), vmem(8 * SLOTS, BW)]
    if len(theirs) == 2:
        work += [vmem(2 * part_rows(below), BW)]
    return pl.pallas_call(
        functools.partial(merge_kernel, levels, level),
        out_shape=out,
        in_specs=[SCALARS, SCALARS, WHOLE] + [WHOLE] * (len(theirs) + len(ahead)),
        out_specs=(WHOLE,) * len(out),
        scratch_shapes=work,
        compiler_params=PARAMS,
        name=f"merge_{level}",
    )(core, plan, own, *ahead, *theirs)


def recover(levels, plan, couplings, reduced, leaf, perm, cells):
    return pl.pallas_call(
        functools.partial(recover_kernel, levels),
        out_shape=(f32(1, FW), f32(1 << levels, BW)),
        in_specs=[SCALARS] + [WHOLE] * (2 * levels + 2),
        out_specs=(WHOLE, WHOLE),
        compiler_params=PARAMS,
        name="recover",
    )(plan, *couplings, *reduced, leaf, perm, cells)


def partner(block, axis, bit):
    count = lax.axis_size(axis)
    return lax.ppermute(block, axis, [(k, k ^ (1 << bit)) for k in range(count)])


def shards(leaf_matrix, leaf_source, observe, zone_ids, log_perm, block_map):
    leaf_count = lax.axis_size("leaf")
    devices = leaf_count * lax.axis_size("sub")
    leaf_bits = leaf_count.bit_length() - 1
    levels = devices.bit_length() - 1
    tree = (lax.axis_index("leaf") + leaf_count * lax.axis_index("sub")).astype(jnp.int32)[None]
    core = tree & 1
    plan = make_plan(levels, tree, block_map)
    zones = jnp.broadcast_to(log_perm[None], (devices, log_perm.shape[0]))
    all_zones = lax.all_to_all(zones, ("leaf", "sub"), 0, 0, tiled=True)
    leaf, pack, perm = leaf_front(levels, plan, leaf_matrix[0], leaf_source, observe, all_zones, zone_ids)
    front, couplings, reduced = leaf, [], []
    for level in range(levels):
        axis, bit = ("leaf", level) if level < leaf_bits else ("sub", level - leaf_bits)
        ahead = ()
        if early(levels, level):
            ahead = (shared_inverse(level, plan, lead, partner(lead, axis, bit)),)
        theirs = (partner(pack, axis, bit),)
        if level > 0 and parts(active(levels, level)) == 2:
            if ahead:
                theirs, ahead = lax.optimization_barrier((theirs, ahead))
            theirs += (partner(theirs[0], "leaf", 0),)
        more = list(merge(levels, level, core, plan, front, theirs, ahead))
        if early(levels, level + 1):
            lead = more.pop(0)
        if level < levels - 1:
            *more, front, pack = more
        couplings += more[:-1]
        reduced += more[-1:]
    solution, partial = recover(levels, plan, couplings, reduced, leaf, perm, zone_ids)
    shares = lax.all_to_all(partial, ("leaf", "sub"), 0, 0, tiled=True)
    return solution, shares.sum(0)


def solution(mesh):
    split_all = ("leaf", "sub")
    in_specs = (P(split_all, None, None), P(split_all, None), P(split_all, None), P(split_all, None), P(split_all), P())
    out_specs = (P(split_all, None), P(split_all))
    return jax.shard_map(shards, mesh=mesh, in_specs=in_specs, out_specs=out_specs, check_vma=False)
```

```python
import functools

import jax
import jax.numpy as jnp
from jax import lax
from jax.experimental import pallas as pl
from jax.experimental.pallas import tpu as pltpu
from jax.sharding import PartitionSpec as P

BW = 128
BW_BITS = 7
NB = 4
KEEP = NB - 1
FW = NB * BW
SLOTS = 64
NEVER = 99
STRIDE = 16
VMEM_LIMIT = 48 * 1024 * 1024


def split(x):
    high = x.astype(jnp.bfloat16)
    return high, (x - high.astype(jnp.float32)).astype(jnp.bfloat16)


def split_exact(x):
    high, low = split(x)
    rest = x - high.astype(jnp.float32)
    return high, low, (rest - low.astype(jnp.float32)).astype(jnp.bfloat16)


def one_hot(cells, width):
    row = lax.broadcasted_iota(jnp.int32, (width, cells.shape[1]), 0)
    return row == jnp.broadcast_to(cells, row.shape)


def dot_split(a, b):
    one = functools.partial(jnp.dot, preferred_element_type=jnp.float32)
    both = one(jnp.concatenate([a[0], a[1]], 1), jnp.concatenate([b[0], b[0]], 0))
    return both + one(a[0], b[1])


def dot_split_left(a, b):
    one = functools.partial(
        lax.dot_general, dimension_numbers=(((0,), (0,)), ((), ())), preferred_element_type=jnp.float32
    )
    both = one(jnp.concatenate([a[0], a[1]], 0), jnp.concatenate([b[0], b[0]], 0))
    return both + one(a[0], b[1])


def dot_split_right(a, b):
    one = functools.partial(
        lax.dot_general, dimension_numbers=(((1,), (1,)), ((), ())), preferred_element_type=jnp.float32
    )
    both = one(jnp.concatenate([a[0], a[1]], 1), jnp.concatenate([b[0], b[0]], 1))
    return both + one(a[0], b[1])


def lanes(x, c):
    return jnp.broadcast_to(x[:, c : c + 1], (8, BW))


def rows(x, j):
    return jnp.broadcast_to(x[j : j + 1, :], (8, BW))


def pivots(row, cols, sub, buffer, slot):
    def pair(v, j):
        slot[0] = (slot[0] + 1) % SLOTS
        at = 8 * slot[0]
        buffer[at : at + 8, :] = v
        return [jnp.broadcast_to(buffer[at + i : at + i + 1, :], (8, BW)) for i in (j, j + 1)]

    for j in range(0, 8, 2):
        left, right = cols[j], cols[j + 1]
        spread = {m: pair(cols[m], j) for m in range(j, 8)}
        a, b, c = spread[j][0], spread[j][1], spread[j + 1][1]
        scale = 1.0 / (a * c - b * b)
        first, second = sub == j, sub == j + 1

        def update(v, v0, v1):
            u0 = c * v0 - b * v1
            u1 = a * v1 - b * v0
            t = left * u0 + right * u1
            return jnp.where(first, u0 * scale, jnp.where(second, u1 * scale, v - t * scale))

        row = update(row, *pair(row, j))
        for m in range(j + 2, 8):
            cols[m] = update(cols[m], *spread[m])
    return row


def invert(slabs, buffer):
    lane = lax.broadcasted_iota(jnp.int32, (8, BW), 1)
    sub = lax.broadcasted_iota(jnp.int32, (8, BW), 0)
    slabs = list(slabs)
    count = len(slabs)
    half = count // 2
    slot = [0]
    for panel in (range(half), range(half, count)):
        for k in panel:
            cols = [lanes(slabs[k], 8 * k + j) for j in range(8)]
            inside = (lane >= 8 * k) & (lane < 8 * k + 8)
            row = jnp.where(lane == sub + 8 * k, 1.0, jnp.where(inside, 0.0, slabs[k]))
            row = pivots(row, cols, sub, buffer, slot)
            w = [rows(row, j) for j in range(8)]
            for r in [r for r in panel if r > k] + [r for r in panel if r < k]:
                t0 = jnp.where(inside, 0.0, slabs[r]) - lanes(slabs[r], 8 * k) * w[0]
                t1 = lanes(slabs[r], 8 * k + 1) * w[1]
                for j in range(2, 8, 2):
                    t0 = t0 - lanes(slabs[r], 8 * k + j) * w[j]
                    t1 = t1 + lanes(slabs[r], 8 * k + j + 1) * w[j + 1]
                slabs[r] = t0 - t1
            slabs[k] = row
        start, stop = 8 * panel[0], 8 * panel[-1] + 8
        inside = (lane >= start) & (lane < stop)
        rest = [r for r in range(count) if r not in panel]
        g = jnp.concatenate([slabs[r][:, start:stop] for r in rest], 0)
        change = dot_split(split(g), split(jnp.concatenate([slabs[r] for r in panel], 0)))
        for n, r in enumerate(rest):
            slabs[r] = jnp.where(inside, 0.0, slabs[r]) - change[8 * n : 8 * n + 8]
    return slabs


def span(block):
    return pl.ds(pl.multiple_of(block * BW, BW), BW)


def invert_ref(load, store, buffer):
    out = invert([load(8 * r) for r in range(BW // 8)], buffer)
    for r in range(BW // 8):
        store[8 * r : 8 * r + 8, :] = out[r]


def sweep(front, inverse, wide, buffer, block):
    at = pl.multiple_of(block * BW, BW)
    invert_ref(lambda r: front[pl.ds(at + r, 8), pl.ds(at, BW)], inverse, buffer)
    wide[...] = dot_split(split(inverse[...]), split(front[pl.ds(at, BW), :]))
    wide[:, pl.ds(at, BW)] = inverse[...]
    w = split(wide[...])
    for start, size in [(i * BW, BW) for i in range(NB)] + [(FW, 8)]:
        g = split(front[start : start + size, pl.ds(at, BW)])
        front[start : start + size, pl.ds(at, BW)] = jnp.zeros((size, BW), jnp.float32)
        front[start : start + size, :] -= dot_split(g, w)


def active(levels, level):
    return min(NB, levels - level)


def pairs(count):
    return [(a, b) for a in range(count) for b in range(a, count)]


def parts(count):
    return 1 if count * (count + 1) // 2 % 2 else 2


def part_rows(count):
    return len(pairs(count)) // parts(count) * BW + -(-count // parts(count)) * 8


def block_row(count, p):
    each = len(pairs(count)) // parts(count)
    return p // each * part_rows(count) + p % each * BW


def rhs_row(count, a):
    each = -(-count // parts(count))
    return a // each * part_rows(count) + len(pairs(count)) // parts(count) * BW + a % each * 8


def write_pack(front, pack, count, core, at, rhs, valid):
    size = part_rows(count)
    whole = pack.shape[0] == parts(count) * size

    def put(start, height, source, ok):
        part = start // size
        to = start if whole else start % size
        ok = ok if whole else ok & (core == part)

        @pl.when(ok)
        def _():
            pack[to : to + height, :] = source()

    for p, (a, b) in enumerate(pairs(count)):
        put(block_row(count, p), BW, lambda a=a, b=b: front[at(a), at(b)], valid(a) & valid(b))
    for a in range(count):
        put(rhs_row(count, a), 8, lambda a=a: front[rhs : rhs + 8, at(a)], valid(a))


def plan_kernel(levels, tree_ref, map_ref, plan, when, position):
    tree = tree_ref[0]
    for i in range(NB):
        when[levels * NB + i] = NEVER
        position[levels * NB + i] = -1
    for level in reversed(range(levels)):
        nodes, node = (1 << levels) >> level, tree >> level
        mine, yours = (
            [map_ref[(nodes + n - 2) * NB + i] for i in range(NB)] for n in (node, node ^ 1)
        )
        dropped = active(levels, level + 1)
        for child, other, base in ((mine, yours, 0), (yours, mine, 4)):
            after, spot, place = [], [], []
            for m in child:
                both = functools.reduce(jnp.logical_or, [m == o for o in other])
                above = (level + 1) * NB + jnp.maximum(m - KEEP, 0)
                later = jnp.where(m >= KEEP, when[above], NEVER)
                after.append(jnp.where(both, level, later))
                place.append(jnp.where(later < NEVER, position[above], jnp.where(both, dropped, -1)))
            for i in range(NB):
                ahead = functools.reduce(jnp.add, [jnp.where(after[k] < after[i], 1, 0) for k in range(NB) if k != i])
                spot.append(jnp.where(after[i] < NEVER, ahead, -1))
            for a in range(NB):
                slot, order = jnp.int32(-1), jnp.int32(-1)
                for i in range(NB):
                    slot = jnp.where(spot[i] == a, place[i], slot)
                    order = jnp.where(spot[i] == a, i, order)
                plan[level * STRIDE + base + a] = slot
                if level == 0 and base == 0:
                    plan[levels * STRIDE + a] = order
            if base == 0:
                for i in range(NB):
                    when[level * NB + i] = after[i]
                    position[level * NB + i] = spot[i]
                    if level == 0:
                        plan[levels * STRIDE + 4 + i] = spot[i]
        plan[level * STRIDE + 8] = jnp.where(plan[level * STRIDE] == dropped, 1, 0)


def leaf_kernel(levels, plan, leaf, source, observe, zones, cells, front, pack, perm, inverse, wide, buffer):
    owner = one_hot(cells[...] >> BW_BITS, zones.shape[0]).astype(jnp.float32).astype(jnp.bfloat16)
    held = sum(
        lax.dot_general(part, owner, (((0,), (0,)), ((), ())), preferred_element_type=jnp.float32)
        for part in split_exact(zones[...])
    )
    within = one_hot(cells[...] & (BW - 1), BW)
    perm[...] = jnp.exp(jnp.sum(jnp.where(within, held, 0.0), axis=0, keepdims=True))
    front[0:FW, :] = leaf[...]
    eye = lax.broadcasted_iota(jnp.int32, (BW, BW), 0) == lax.broadcasted_iota(jnp.int32, (BW, BW), 1)
    for i in range(NB):
        at = slice(i * BW, i * BW + BW)
        front[at, at] += jnp.where(eye, jnp.broadcast_to(perm[:, at], (BW, BW)), 0.0)
    which = lax.broadcasted_iota(jnp.int32, (8, FW), 0)
    front[FW : FW + 8, :] = jnp.where(
        which == 0,
        jnp.broadcast_to(source[...], (8, FW)),
        jnp.where(which == 1, jnp.broadcast_to(observe[...], (8, FW)), 0.0),
    )
    order = [plan[levels * STRIDE + a] for a in range(NB)]

    def step(i, carry):
        @pl.when(plan[levels * STRIDE + 4 + i] < 0)
        def _():
            sweep(front, inverse, wide, buffer, i)

        return carry

    lax.fori_loop(0, NB, step, 0)
    count = active(levels, 0)
    write_pack(
        front, pack, count, 0, lambda a: span(jnp.maximum(order[a], 0)), FW, lambda a: order[a] >= 0
    )


def inverse_kernel(level, plan, own, theirs, inverse, buffer):
    @pl.when(plan[level * STRIDE + 8] == 1)
    def _():
        inverse[...] = own[...] + theirs[...]
        invert_ref(lambda r: inverse[r : r + 8, :], inverse, buffer)


def early(levels, level):
    return False


def merge_kernel(levels, level, core_ref, plan, own, *rest):
    if early(levels, level):
        ahead, *rest = rest
    below, count = active(levels, level), active(levels, level + 1)
    core = core_ref[0]
    base = level * STRIDE
    if level > 0 and parts(below) == 2:
        same, swapped, *rest, theirs = rest
        size = part_rows(below)
        theirs[pl.ds(pl.multiple_of(core * size, 8), size), :] = same[...]
        theirs[pl.ds(pl.multiple_of((1 - core) * size, 8), size), :] = swapped[...]
    else:
        theirs, *rest = rest
    if not early(levels, level):
        *rest, ahead, buffer = rest
    if early(levels, level + 1):
        lead, *rest = rest
    if count:
        coupling, reduced, front, pack, diagonal, coupled = rest
        front[...] = jnp.zeros(front.shape, jnp.float32)
        coupled[...] = jnp.zeros(coupled.shape, jnp.float32)
    else:
        reduced, diagonal = rest
    mine = [plan[base + a] for a in range(below)]
    yours = [plan[base + 4 + a] for a in range(below)]
    eliminated = plan[base + 8] == 1
    kept = plan[base + 8] == 0
    rhs = count * BW
    if level == 0:
        order = [jnp.maximum(plan[levels * STRIDE + a], 0) for a in range(below)]
        at, own_rhs = lambda a: span(order[a]), FW
    else:
        at, own_rhs = lambda a: slice(a * BW, a * BW + BW), below * BW
    their_rows = {p: block_row(below, n) for n, p in enumerate(pairs(below))}
    their_block = lambda a, b: theirs[their_rows[a, b] : their_rows[a, b] + BW, :]
    their_rhs = lambda a: theirs[rhs_row(below, a) : rhs_row(below, a) + 8, :]
    diagonal[...] = own[at(0), at(0)] + their_block(0, 0)
    right = own[own_rhs : own_rhs + 8, at(0)] + their_rhs(0)
    reduced[...] = right

    def put(ok, a, b, value):
        @pl.when(ok)
        def _():
            front[span(a), span(b)] = value()

    def put_rhs(ok, a, value):
        @pl.when(ok)
        def _():
            front[rhs : rhs + 8, span(a)] = value()

    if count:
        put(kept, mine[0], mine[0], lambda: diagonal[...])
        put_rhs(kept, mine[0], lambda: reduced[...])
        for a in range(1, below):
            for slots, block, across, vector in (
                (mine, lambda a, b: own[at(a), at(b)], lambda a, b: own[at(b), at(a)], lambda a: own[own_rhs : own_rhs + 8, at(a)]),
                (yours, their_block, lambda a, b: their_block(a, b).T, their_rhs),
            ):
                there = slots[a] >= 0

                @pl.when(there & eliminated)
                def _():
                    coupled[:, span(slots[a])] = block(0, a)

                put(there & kept, slots[0], slots[a], lambda: block(0, a))
                put(there & kept, slots[a], slots[0], lambda: across(0, a))
                put_rhs(there, slots[a], lambda: vector(a))
                for b in range(a, below):
                    both = there & (slots[b] >= 0)
                    put(both, slots[a], slots[b], lambda: block(a, b))
                    if a != b:
                        put(both, slots[b], slots[a], lambda: across(a, b))

    @pl.when(eliminated)
    def _():
        if not early(levels, level):
            invert_ref(lambda r: diagonal[r : r + 8, :], ahead, buffer)
        d, r = split(ahead[...]), split(reduced[...])
        if count:
            c = split(coupled[...])
            w = dot_split(d, c)
            coupling[...] = w
            w = split(w)
            front[0:rhs, :] -= dot_split_left(c, w)
            front[rhs : rhs + 8, :] -= dot_split(r, w)
        reduced[...] = dot_split(r, d)

    if count:

        @pl.when(kept)
        def _():
            coupling[...] = jnp.zeros(coupling.shape, jnp.float32)

        write_pack(
            front, pack, count, core, lambda a: slice(a * BW, a * BW + BW), rhs, lambda a: plan[0] == plan[0]
        )
        if early(levels, level + 1):
            lead[...] = front[0:BW, 0:BW]


def pick(blocks, slot):
    out = jnp.zeros((8, BW), jnp.float32)
    for n, block in enumerate(blocks):
        out = jnp.where(slot == n, block, out)
    return out


def recover_kernel(levels, plan, *refs):
    couplings, reduced = refs[: levels - 1], refs[levels - 1 : 2 * levels - 1]
    leaf, perm, cells, out, partial = refs[2 * levels - 1 :]
    solved = [reduced[levels - 1][...]]
    for level in reversed(range(1, levels)):
        kept = [pick(solved, plan[level * STRIDE + a]) for a in range(active(levels, level))]
        z = split(jnp.concatenate(kept, 1))
        solved = kept + [reduced[level - 1][...] - dot_split_right(z, split(couplings[level - 1][...]))]
    spots = [plan[levels * STRIDE + 4 + i] for i in range(NB)]
    kept = [pick(solved, jnp.where(spot >= 0, plan[jnp.maximum(spot, 0)], -1)) for spot in spots]
    new = dot_split(split(jnp.concatenate(kept, 1)), split(leaf[0:FW, :])) - leaf[FW : FW + 8, :]
    both = jnp.concatenate(
        [jnp.where(spots[i] >= 0, kept[i], new[:, i * BW : i * BW + BW]) for i in range(NB)], 1
    )
    out[...] = both[0:1]
    terms = -perm[...] * both[0:1] * both[1:2]
    owner = one_hot(cells[...] >> BW_BITS, partial.shape[0]).astype(jnp.float32).astype(jnp.bfloat16)
    within = one_hot(cells[...] & (BW - 1), BW)
    spread = jnp.where(within, jnp.broadcast_to(terms, within.shape), 0.0)
    partial[...] = sum(
        lax.dot_general(owner, part, (((1,), (1,)), ((), ())), preferred_element_type=jnp.float32)
        for part in split_exact(spread)
    )


SCALARS = pl.BlockSpec(memory_space=pltpu.SMEM)
WHOLE = pl.BlockSpec(memory_space=pltpu.VMEM)
PARAMS = pltpu.CompilerParams(vmem_limit_bytes=VMEM_LIMIT)
LEAF_PARAMS = pltpu.CompilerParams(vmem_limit_bytes=62 * 1024 * 1024)


def f32(*shape):
    return jax.ShapeDtypeStruct(shape, jnp.float32)


def vmem(*shape):
    return pltpu.VMEM(shape, jnp.float32)


def make_plan(levels, tree, maps):
    return pl.pallas_call(
        functools.partial(plan_kernel, levels),
        out_shape=jax.ShapeDtypeStruct(((levels + 1) * STRIDE,), jnp.int32),
        in_specs=[SCALARS, SCALARS],
        out_specs=SCALARS,
        scratch_shapes=[pltpu.SMEM(((levels + 1) * NB,), jnp.int32)] * 2,
        name="make_plan",
    )(tree, maps)


def leaf_front(levels, plan, leaf, source, observe, zones, cells):
    count = active(levels, 0)
    return pl.pallas_call(
        functools.partial(leaf_kernel, levels),
        out_shape=(f32(FW + 8, FW), f32(parts(count) * part_rows(count), BW), f32(1, FW)),
        in_specs=[SCALARS] + [WHOLE] * 5,
        out_specs=(WHOLE,) * 3,
        scratch_shapes=[vmem(BW, BW), vmem(BW, FW), vmem(8 * SLOTS, BW)],
        compiler_params=LEAF_PARAMS,
        name="leaf_front",
    )(plan, leaf, source, observe, zones, cells)


def shared_inverse(level, plan, own, theirs):
    return pl.pallas_call(
        functools.partial(inverse_kernel, level),
        out_shape=f32(BW, BW),
        in_specs=[SCALARS, WHOLE, WHOLE],
        out_specs=WHOLE,
        scratch_shapes=[vmem(8 * SLOTS, BW)],
        compiler_params=PARAMS,
        cost_estimate=pl.CostEstimate(flops=4 * BW**3, bytes_accessed=12 * BW * BW, transcendentals=0),
        name=f"inverse_{level}",
    )(plan, own, theirs)


def merge(levels, level, core, plan, own, theirs, ahead):
    below, count = active(levels, level), active(levels, level + 1)
    n = count * BW
    out, work = (f32(8, BW),), [vmem(BW, BW)]
    if count:
        out = (f32(BW, n),) + out + (f32(n + 8, n), f32(part_rows(count), BW))
        work += [vmem(BW, n)]
    if early(levels, level + 1):
        out = (f32(BW, BW),) + out
    if not early(levels, level):
        work += [vmem(BW, BW), vmem(8 * SLOTS, BW)]
    if len(theirs) == 2:
        work += [vmem(2 * part_rows(below), BW)]
    return pl.pallas_call(
        functools.partial(merge_kernel, levels, level),
        out_shape=out,
        in_specs=[SCALARS, SCALARS, WHOLE] + [WHOLE] * (len(theirs) + len(ahead)),
        out_specs=(WHOLE,) * len(out),
        scratch_shapes=work,
        compiler_params=PARAMS,
        name=f"merge_{level}",
    )(core, plan, own, *ahead, *theirs)


def recover(levels, plan, couplings, reduced, leaf, perm, cells):
    return pl.pallas_call(
        functools.partial(recover_kernel, levels),
        out_shape=(f32(1, FW), f32(1 << levels, BW)),
        in_specs=[SCALARS] + [WHOLE] * (2 * levels + 2),
        out_specs=(WHOLE, WHOLE),
        compiler_params=PARAMS,
        name="recover",
    )(plan, *couplings, *reduced, leaf, perm, cells)


def partner(block, axis, bit):
    count = lax.axis_size(axis)
    return lax.ppermute(block, axis, [(k, k ^ (1 << bit)) for k in range(count)])


def shards(leaf_matrix, leaf_source, observe, zone_ids, log_perm, block_map):
    leaf_count = lax.axis_size("leaf")
    devices = leaf_count * lax.axis_size("sub")
    leaf_bits = leaf_count.bit_length() - 1
    levels = devices.bit_length() - 1
    tree = (lax.axis_index("leaf") + leaf_count * lax.axis_index("sub")).astype(jnp.int32)[None]
    core = tree & 1
    plan = make_plan(levels, tree, block_map.reshape(-1))
    zones = jnp.broadcast_to(log_perm[None], (devices, log_perm.shape[0]))
    all_zones = lax.all_to_all(zones, ("leaf", "sub"), 0, 0, tiled=True)
    leaf, pack, perm = leaf_front(levels, plan, leaf_matrix[0], leaf_source, observe, all_zones, zone_ids)
    front, couplings, reduced = leaf, [], []
    for level in range(levels):
        axis, bit = ("leaf", level) if level < leaf_bits else ("sub", level - leaf_bits)
        ahead = ()
        if early(levels, level):
            ahead = (shared_inverse(level, plan, lead, partner(lead, axis, bit)),)
        theirs = (partner(pack, axis, bit),)
        if level > 0 and parts(active(levels, level)) == 2:
            if ahead:
                theirs, ahead = lax.optimization_barrier((theirs, ahead))
            theirs += (partner(theirs[0], "leaf", 0),)
        more = list(merge(levels, level, core, plan, front, theirs, ahead))
        if early(levels, level + 1):
            lead = more.pop(0)
        if level < levels - 1:
            *more, front, pack = more
        couplings += more[:-1]
        reduced += more[-1:]
    solution, partial = recover(levels, plan, couplings, reduced, leaf, perm, zone_ids)
    shares = lax.all_to_all(partial, ("leaf", "sub"), 0, 0, tiled=True)
    return solution, shares.sum(0)


def solution(mesh):
    split_all = ("leaf", "sub")
    in_specs = (P(split_all, None, None), P(split_all, None), P(split_all, None), P(split_all, None), P(split_all), P())
    out_specs = (P(split_all, None), P(split_all))
    return jax.shard_map(shards, mesh=mesh, in_specs=in_specs, out_specs=out_specs, check_vma=False)
```
